256 devices in a mesh: prompt: 8 (over z_lo, core), resp: 32 (over x, y, z_hi).
Axes of the slice: x: 4, y: 4, z: 8 (z_hi: 2, z_lo: 4; z = z_hi * 4 + z_lo), core: 2. Of those that a mesh axis runs over, the one named last changes fastest.
Arguments:
- prompt_hidden: bfloat16 [16, 3072, 5120], P('prompt', 'resp'), may hold values from -6 to 6
- prompt_keys: bfloat16 [16, 3072, 128], P('prompt', 'resp'), may hold values from -6 to 6
- prompt_values: bfloat16 [16, 3072, 128], P('prompt', 'resp'), may hold values from -6 to 6
- resp_hidden: bfloat16 [8, 2048, 5120], P('prompt', 'resp'), may hold values from -6 to 6
- resp_queries: bfloat16 [8, 2048, 1024], P('prompt', 'resp'), may hold values from -180 to 180
- resp_keys: bfloat16 [8, 2048, 128], P('prompt', 'resp'), may hold values from -6 to 6
- resp_values: bfloat16 [8, 2048, 128], P('prompt', 'resp'), may hold values from -6 to 6
- cotangent: bfloat16 [8, 2048, 1024], P('prompt', 'resp'), may hold values from -6 to 6
- rewards: float32 [8, 32], P('prompt', 'resp'), may hold values from -4 to 4
- resp_prompt: int32 [8, 32], P('prompt', 'resp'), may hold values from 0 to 1, as said below
- resp_len: int32 [8, 32], P('prompt', 'resp'), may hold values from 1 to 64, as said below
- prompt_tenant: int32 [16], P('prompt'), may hold values from 0 to 7
- q_down: bfloat16 [8, 5120, 16], replicated, may hold values from -0.078125 to 0.078125
- q_up: bfloat16 [8, 16, 1024], replicated, may hold values from -1.5 to 1.5
- v_down: bfloat16 [8, 5120, 16], replicated, may hold values from -0.078125 to 0.078125
- v_up: bfloat16 [8, 16, 128], replicated, may hold values from -1.5 to 1.5
Outputs:
- attn_out: bfloat16 [8, 2048, 1024], P('prompt', 'resp')
- grad_q_down: float32 [8, 5120, 16], replicated
- grad_q_up: float32 [8, 16, 1024], replicated
- grad_v_down: float32 [8, 5120, 16], replicated
- grad_v_up: float32 [8, 16, 128], replicated
The draws below stay inside these ranges and needn't reach their ends.
Inputs may be any that keep to these rules, and one draw needn't show every extreme that they name: `resp_len`: in every group one response has exactly 64 tokens; slots at or beyond a response's length are padding. `resp_prompt`: in one group every response continues prompt 1; in every other group some response continues prompt 0.
All inputs are finite; a program needn't handle non-finite values.
Results may differ from the reference program's by a relative error of at most 0.023.
Values may be sent and summed in bfloat16 or wider, within the bound.
A program may use at most 256 MiB of HBM per device.

```python
import jax
import jax.numpy as jnp
from jax import lax

D = 5120
HD = 128
HQ = 8
RANK = 16
TENANTS = 8
PR_DEV = 2
RLEN = 64
NR = 32
GROUPS = 8
PROMPTS = 16
PLEN = 3072
RTOK = 2048


def draw_resp_len(key, part):
    key = jax.random.fold_in(key, 7)
    first_key, second_key = jax.random.split(key)
    drawn = jax.random.randint(first_key, (GROUPS, NR), 1, RLEN + 1)
    longest = jax.random.randint(second_key, (GROUPS, 1), 0, NR)
    return jnp.where(jnp.arange(NR)[None, :] == longest, RLEN, drawn).astype(jnp.int32)


def draw_resp_prompt(key, part):
    key = jax.random.fold_in(key, 13)
    first_key, second_key, third_key = jax.random.split(key, 3)
    drawn = jax.random.randint(first_key, (GROUPS, NR), 0, PR_DEV)
    anchor = jax.random.randint(second_key, (GROUPS, 1), 0, NR)
    drawn = jnp.where(jnp.arange(NR)[None, :] == anchor, 0, drawn)
    single = jax.random.randint(third_key, (), 0, GROUPS)
    return jnp.where(jnp.arange(GROUPS)[:, None] == single, PR_DEV - 1, drawn).astype(jnp.int32)


def draw_prompt_keys(key, part):
    key = jax.random.fold_in(key, 11)
    noise_key = jax.random.fold_in(key, 0)
    noisy = jnp.clip(jax.random.normal(noise_key, (PROMPTS, PLEN, HD), jnp.float32), -6.0, 6.0)
    return noisy.astype(jnp.bfloat16)


def draw_resp_queries(key, part):
    key = jax.random.fold_in(key, 17)
    noise_key = jax.random.fold_in(key, 0)
    noisy = jnp.clip(jax.random.normal(noise_key, (GROUPS, RTOK, HQ * HD), jnp.float32), -6.0, 6.0)
    return noisy.astype(jnp.bfloat16)


def set_ends(array, own_key, low, largest):
    index_at = [jax.random.randint(jax.random.fold_in(own_key, axis), (), 0, length) for axis, length in enumerate(array.shape)]
    widest = array.shape.index(max(array.shape))
    neighbour = index_at[:widest] + [(index_at[widest] + 1) % array.shape[widest]] + index_at[widest + 1:]
    return array.at[tuple(index_at)].set(low).at[tuple(neighbour)].set(largest)


def block_levels(rng, dims, shards, low, high):
    gain = 1.0
    for axis_at, blocks in shards:
        draws = jax.random.uniform(jax.random.fold_in(jax.random.fold_in(rng, 6), axis_at), (blocks,), jnp.float32, low / len(shards), high / len(shards))
        gain = gain * jnp.repeat(jnp.exp(draws), dims[axis_at] // blocks).reshape((-1,) + (1,) * (len(dims) - 1 - axis_at))
    return gain


def normal_values(rng, extent, scale, reach, cuts=(), dtype=jnp.bfloat16):
    level = block_levels(rng, extent, cuts, -0.22, 0.18) if cuts else 1.0
    values = jax.random.normal(rng, extent, jnp.float32) * scale * level
    return jnp.minimum(jnp.maximum(values, -reach), reach).astype(dtype)


def setup_inputs(seed: int = 0) -> dict:
    arg_keys = jax.random.split(jax.random.key(seed), 17)
    return {
        "prompt_hidden": normal_values(arg_keys[0], (PROMPTS, PLEN, D), 1.0, 6.0, ((0, 8), (1, 32))),
        "prompt_keys": draw_prompt_keys(jax.random.fold_in(arg_keys[16], 71), 0),
        "prompt_values": normal_values(arg_keys[2], (PROMPTS, PLEN, HD), 1.0, 6.0, ((0, 8), (1, 32))),
        "resp_hidden": normal_values(arg_keys[3], (GROUPS, RTOK, D), 1.0, 6.0, ((0, 8), (1, 32))),
        "resp_queries": draw_resp_queries(jax.random.fold_in(arg_keys[16], 71), 0),
        "resp_keys": normal_values(arg_keys[5], (GROUPS, RTOK, HD), 1.0, 6.0, ((0, 8), (1, 32))),
        "resp_values": normal_values(arg_keys[6], (GROUPS, RTOK, HD), 1.0, 6.0, ((0, 8), (1, 32))),
        "cotangent": normal_values(arg_keys[7], (GROUPS, RTOK, HQ * HD), 1.0, 6.0, ((0, 8), (1, 32))),
        "rewards": normal_values(arg_keys[8], (GROUPS, NR), 1.0, 4.0, ((0, 8), (1, 32)), jnp.float32),
        "resp_prompt": draw_resp_prompt(jax.random.fold_in(arg_keys[16], 71), 0),
        "resp_len": draw_resp_len(jax.random.fold_in(arg_keys[16], 71), 0),
        "prompt_tenant": set_ends(jax.random.randint(arg_keys[11], (PROMPTS,), 0, TENANTS), jax.random.fold_in(arg_keys[11], 1), 0, TENANTS - 1).astype(jnp.int32),
        "q_down": normal_values(arg_keys[12], (TENANTS, D, RANK), D ** -0.5, 0.078125),
        "q_up": normal_values(arg_keys[13], (TENANTS, RANK, HQ * HD), RANK ** -0.5, 1.5),
        "v_down": normal_values(arg_keys[14], (TENANTS, D, RANK), D ** -0.5, 0.078125),
        "v_up": normal_values(arg_keys[15], (TENANTS, RANK, HD), RANK ** -0.5, 1.5),
    }


adapter_scale = 2.0
contract_rows = (((0,), (0,)), ((), ()))


def lift_values(hidden_rows, frozen_output, down, up_projection):
    low_rank_rows = jnp.dot(hidden_rows, down, preferred_element_type=jnp.float32).astype(jnp.bfloat16)
    adapter_output = frozen_output.astype(jnp.float32) + adapter_scale * jnp.dot(low_rank_rows, up_projection, preferred_element_type=jnp.float32)
    return low_rank_rows, adapter_output.astype(jnp.bfloat16)


def prompt_terms(hidden_rows, low_rank_rows, values_gradient, up_projection):
    hidden_prompt = lax.Precision.HIGHEST
    up_gradient = adapter_scale * jnp.dot(low_rank_rows.astype(jnp.float32).T, values_gradient, precision=hidden_prompt)
    backward_result = jnp.dot(values_gradient, up_projection.astype(jnp.float32).T, precision=hidden_prompt).astype(jnp.bfloat16)
    down_gradient = adapter_scale * jnp.dot(hidden_rows.T, backward_result, preferred_element_type=jnp.float32)
    return down_gradient, up_gradient


def respond(response_input, frozen_query_rows, base_key, base_value, upstream_raw, keys_p, values_p, length, weight, a_query, query_up_matrix, a_value, b_value):
    slots = response_input.shape[0]
    head_dim = base_key.shape[1]
    heads = frozen_query_rows.shape[1] // head_dim
    factor = head_dim ** -0.5
    query_low_rank = jnp.dot(response_input, a_query, preferred_element_type=jnp.float32).astype(jnp.bfloat16)
    query_rows = (frozen_query_rows.astype(jnp.float32) + adapter_scale * jnp.dot(query_low_rank, query_up_matrix, preferred_element_type=jnp.float32)).astype(jnp.bfloat16)
    value_low_rank, own_values = lift_values(response_input, base_value, a_value, b_value)
    q_rows = query_rows.reshape(slots * heads, head_dim)
    score_p = jnp.dot(q_rows, keys_p.T, preferred_element_type=jnp.float32) * factor
    score_s = jnp.dot(q_rows, base_key.T, preferred_element_type=jnp.float32) * factor
    q_pos = jnp.arange(slots * heads) // heads
    k_pos = jnp.arange(slots)
    allowed = (k_pos[None, :] <= q_pos[:, None]) & (k_pos[None, :] < length)
    highest = jnp.maximum(jnp.max(score_p, axis=1), jnp.max(jnp.where(allowed, score_s, -1e30), axis=1))[:, None]
    exp_p = jnp.exp(score_p - highest)
    exp_s = jnp.where(allowed, jnp.exp(score_s - highest), 0.0)
    totals = (jnp.sum(exp_p, axis=1) + jnp.sum(exp_s, axis=1))[:, None]
    prob_p = exp_p / totals
    prob_s = exp_s / totals
    weight_p = prob_p.astype(jnp.bfloat16)
    weight_s = prob_s.astype(jnp.bfloat16)
    attended = jnp.dot(weight_p, values_p, preferred_element_type=jnp.float32) + jnp.dot(weight_s, own_values, preferred_element_type=jnp.float32)
    live = (jnp.arange(slots) < length).astype(jnp.float32)
    upstream = (upstream_raw.astype(jnp.float32) * (weight * live)[:, None]).astype(jnp.bfloat16).reshape(slots * heads, head_dim)
    delta = jnp.sum(upstream.astype(jnp.float32) * attended, axis=1, keepdims=True)
    grad_sp = (prob_p * (jnp.dot(upstream, values_p.T, preferred_element_type=jnp.float32) - delta)).astype(jnp.bfloat16)
    grad_ss = (prob_s * (jnp.dot(upstream, own_values.T, preferred_element_type=jnp.float32) - delta)).astype(jnp.bfloat16)
    query_gradient = ((jnp.dot(grad_sp, keys_p, preferred_element_type=jnp.float32) + jnp.dot(grad_ss, base_key, preferred_element_type=jnp.float32)) * factor).astype(jnp.bfloat16).reshape(slots, heads * head_dim)
    grad_pv = lax.dot_general(weight_p, upstream, contract_rows, preferred_element_type=jnp.float32)
    attention_output_gradient = lax.dot_general(weight_s, upstream, contract_rows, preferred_element_type=jnp.float32).astype(jnp.bfloat16)
    query_up_gradient = adapter_scale * jnp.dot(query_low_rank.T, query_gradient, preferred_element_type=jnp.float32)
    query_backward = jnp.dot(query_gradient, query_up_matrix.T, preferred_element_type=jnp.float32).astype(jnp.bfloat16)
    query_down_gradient = adapter_scale * jnp.dot(response_input.T, query_backward, preferred_element_type=jnp.float32)
    value_up_gradient = adapter_scale * jnp.dot(value_low_rank.T, attention_output_gradient, preferred_element_type=jnp.float32)
    value_backward = jnp.dot(attention_output_gradient, b_value.T, preferred_element_type=jnp.float32).astype(jnp.bfloat16)
    value_down_gradient = adapter_scale * jnp.dot(response_input.T, value_backward, preferred_element_type=jnp.float32)
    return attended.astype(jnp.bfloat16).reshape(slots, heads * head_dim), grad_pv, query_down_gradient, query_up_gradient, value_down_gradient, value_up_gradient


def reference(prompt_hidden, prompt_keys, prompt_values, resp_hidden, resp_queries, resp_keys, resp_values, cotangent, rewards, resp_prompt, resp_len, prompt_tenant, q_down, q_up, v_down, v_up):
    hidden_prompt = lax.Precision.HIGHEST
    tenant_ids = jnp.arange(TENANTS)
    prompt_ids = jnp.arange(PR_DEV)
    xs = (prompt_hidden.reshape(GROUPS, PR_DEV, PLEN, D), prompt_keys.reshape(GROUPS, PR_DEV, PLEN, HD), prompt_values.reshape(GROUPS, PR_DEV, PLEN, HD), resp_hidden.reshape(GROUPS, NR, RLEN, D), resp_queries.reshape(GROUPS, NR, RLEN, HQ * HD), resp_keys.reshape(GROUPS, NR, RLEN, HD), resp_values.reshape(GROUPS, NR, RLEN, HD), cotangent.reshape(GROUPS, NR, RLEN, HQ * HD), rewards, resp_prompt, resp_len, prompt_tenant.reshape(GROUPS, PR_DEV))

    def one_group(carry, group):
        p_hidden, p_keys, p_values, r_hidden, r_queries, r_keys, r_values, r_cot, r_reward, r_prompt, r_len, p_tenant = group
        lowered_all = []
        lifted_all = []
        for slot in range(PR_DEV):
            low_rank_rows, lifted = lift_values(p_hidden[slot], p_values[slot], v_down[p_tenant[slot]], v_up[p_tenant[slot]])
            lowered_all.append(low_rank_rows)
            lifted_all.append(lifted)
        lifted_stack = jnp.stack(lifted_all)
        picked = (r_prompt[:, None] == prompt_ids[None, :]).astype(jnp.float32)
        sums = jnp.dot(r_reward, picked, precision=hidden_prompt)
        counts = jnp.sum(picked, axis=0)
        means = sums / jnp.maximum(counts, 1.0)
        advantage = r_reward - jnp.dot(picked, means, precision=hidden_prompt)
        weight = -advantage / RLEN
        r_tenant = p_tenant[r_prompt]
        mapped = (r_hidden, r_queries, r_keys, r_values, r_cot, p_keys[r_prompt], lifted_stack[r_prompt], r_len, weight, q_down[r_tenant], q_up[r_tenant], v_down[r_tenant], v_up[r_tenant])
        attn, grad_pv, query_down_gradient, query_up_gradient, value_down_gradient, value_up_gradient = lax.map(lambda item: respond(*item), mapped)
        value_grads = jnp.einsum("rc,rph->cph", picked, grad_pv, precision=hidden_prompt)
        r_onehot = (r_tenant[:, None] == tenant_ids[None, :]).astype(jnp.float32)
        p_onehot = (p_tenant[:, None] == tenant_ids[None, :]).astype(jnp.float32)
        sum_aq = jnp.einsum("rt,rdk->tdk", r_onehot, query_down_gradient, precision=hidden_prompt)
        sum_bq = jnp.einsum("rt,rkf->tkf", r_onehot, query_up_gradient, precision=hidden_prompt)
        sum_av = jnp.einsum("rt,rdk->tdk", r_onehot, value_down_gradient, precision=hidden_prompt)
        sum_bv = jnp.einsum("rt,rkf->tkf", r_onehot, value_up_gradient, precision=hidden_prompt)
        for slot in range(PR_DEV):
            down_term, up_term = prompt_terms(p_hidden[slot], lowered_all[slot], value_grads[slot], v_up[p_tenant[slot]])
            sum_av = sum_av + p_onehot[slot][:, None, None] * down_term[None]
            sum_bv = sum_bv + p_onehot[slot][:, None, None] * up_term[None]
        new_carry = (carry[0] + sum_aq, carry[1] + sum_bq, carry[2] + sum_av, carry[3] + sum_bv)
        return new_carry, attn

    start = (jnp.zeros((TENANTS, D, RANK), jnp.float32), jnp.zeros((TENANTS, RANK, HQ * HD), jnp.float32), jnp.zeros((TENANTS, D, RANK), jnp.float32), jnp.zeros((TENANTS, RANK, HD), jnp.float32))
    totals, attn_all = lax.scan(one_group, start, xs)
    return attn_all.reshape(GROUPS, RTOK, HQ * HD), totals[0], totals[1], totals[2], totals[3]
```

```python
import functools

import jax
import jax.numpy as jnp
from jax import lax
from jax.experimental import pallas as pl
from jax.experimental.pallas import tpu as pltpu
from jax.sharding import PartitionSpec as P

MESH = pl.DeviceIdType.MESH
F32 = jnp.float32
BF16 = jnp.bfloat16
NX = 4
NZ = 8
SIDE = NX * NX
LOG2E = 1.4426950408889634


def dot_nn(a, b):
    return lax.dot_general(a, b, (((1,), (0,)), ((), ())), preferred_element_type=F32)


def dot_nt(a, b):
    return lax.dot_general(a, b, (((1,), (1,)), ((), ())), preferred_element_type=F32)


def dot_tn(a, b):
    return lax.dot_general(a, b, (((0,), (0,)), ((), ())), preferred_element_type=F32)


class Place:
    def __init__(self):
        r = lax.axis_index("resp")
        p = lax.axis_index("prompt")
        self.x = r // 8
        self.y = lax.rem(r // 2, 4)
        self.zh = lax.rem(r, 2)
        self.zl = p // 2
        self.c = lax.rem(p, 2)
        self.z = self.zh * 4 + self.zl
        self.p = self.x * 4 + self.y

    def plane(self, dx, dy):
        x = lax.rem(self.x + dx, 4)
        y = lax.rem(self.y + dy, 4)
        return {"resp": (x * 4 + y) * 2 + self.zh}, x * 4 + y

    def line(self, dz):
        z = lax.rem(self.z + dz, NZ)
        return {
            "prompt": lax.rem(z, 4) * 2 + self.c,
            "resp": self.p * 2 + z // 4,
        }, z

    def other_core(self):
        return {"prompt": self.zl * 2 + (1 - self.c)}

    def along(self, axis, d):
        return self.plane(d, 0)[0] if axis == 0 else self.plane(0, d)[0]


class Spread:
    def __init__(self, at, buf, axis, send, recv, base):
        self.at = at
        self.buf = buf
        self.axis = axis
        self.a = at.x if axis == 0 else at.y
        self.b = at.y if axis == 0 else at.x
        self.send = send
        self.recv = recv
        self.base = base
        self.sent = []

    def copy(self, src, dst, sem, device):
        return pltpu.make_async_remote_copy(
            src_ref=src,
            dst_ref=dst,
            send_sem=self.send.at[self.base + sem],
            recv_sem=self.recv.at[self.base + sem],
            device_id=device,
            device_id_type=MESH,
        )

    def push(self, ref, sem, device):
        c = self.copy(ref, ref, sem, device)
        c.start()
        self.sent.append(c)

    def take(self, ref, sem, device):
        self.copy(ref, ref, sem, device).wait_recv()

    def first(self):
        mine = self.buf.at[self.a, self.b]
        for d in (1, 3, 2):
            self.push(mine, d - 1, self.at.along(1 - self.axis, d))

    def second(self):
        for d in (1, 3, 2):
            self.take(
                self.buf.at[self.a, lax.rem(self.b + 4 - d, 4)],
                d - 1,
                self.at.along(1 - self.axis, d),
            )
        row = self.buf.at[self.a]
        self.push(row, 3, self.at.along(self.axis, 1))
        self.push(row, 4, self.at.along(self.axis, 3))

    def relay(self):
        low = lax.rem(self.a + 3, 4)
        high = lax.rem(self.a + 1, 4)
        self.take(self.buf.at[low], 3, self.at.along(self.axis, 1))
        self.push(self.buf.at[low, pl.ds(0, 2)], 5, self.at.along(self.axis, 1))
        self.take(self.buf.at[high], 4, self.at.along(self.axis, 3))
        self.push(self.buf.at[high, pl.ds(2, 2)], 6, self.at.along(self.axis, 3))

    def finish(self):
        far = lax.rem(self.a + 2, 4)
        self.take(self.buf.at[far, pl.ds(0, 2)], 5, self.at.along(self.axis, 1))
        self.take(self.buf.at[far, pl.ds(2, 2)], 6, self.at.along(self.axis, 3))

    def drain(self):
        for c in self.sent:
            c.wait_send()


SPREAD_SEMS = 7


def step_kernel(
    dims,
    ph_hbm, pk_ref, pv_ref, rh_hbm, rq_ref, rk_ref, rv_ref, cot_ref,
    rew_ref, rp_ref, rl_ref, pt_ref, qd_hbm, qu_ref, vd_hbm, vu_ref,
    attn_ref, gath,
    ph, rh, qd, vd,
    k_own, k_par, v_own, v_par,
    s_scr, e_scr, v_scr, m_scr, l_scr, o_scr, dq_scr,
    stat, stat_in,
    rsb, rsr, bs32, bs16, bz_in,
    g_send, g_in, zbuf, acc32, acc16, core_in, vterm,
    load_sem, sp_send, sp_recv, z_send, z_recv, st_send, st_recv,
    rs_send, rs_recv, bz_sem, g_ssem, g_rsem, zl_ssem, zl_rsem, c_sem, f_sem,
):
    (D, HD, HQ, R, T, PB, RL) = dims
    at = Place()
    rows = RL * HQ
    qtiles = (D + HQ * HD) // HD
    dtiles = D // HD
    per = qtiles // SIDE
    half_t = T // 2

    loads = [
        pltpu.make_async_copy(s, d, load_sem.at[i])
        for i, (s, d) in enumerate(((ph_hbm, ph), (vd_hbm, vd), (rh_hbm, rh), (qd_hbm, qd)))
    ]
    for c in loads:
        c.start()

    barrier = pltpu.get_barrier_semaphore()

    def greet_plane(k, _):
        pl.semaphore_signal(
            barrier, inc=1, device_id=at.plane(k // 4, lax.rem(k, 4))[0], device_id_type=MESH
        )
        return 0

    def greet_line(k, _):
        pl.semaphore_signal(barrier, inc=1, device_id=at.line(k)[0], device_id_type=MESH)
        return 0

    lax.fori_loop(1, SIDE, greet_plane, 0)
    lax.fori_loop(1, NZ, greet_line, 0)
    pl.semaphore_signal(barrier, inc=1, device_id=at.other_core(), device_id_type=MESH)

    for s in range(2):
        a, b = (at.x, at.y) if s == 0 else (at.y, at.x)
        k_own[s, a, b] = pk_ref[s]
        v_own[s, a, b, 0:PB, :] = pv_ref[s]
        v_own[s, a, b, PB : PB + R, :] = jnp.zeros((R, HD), BF16)
    rsb[...] = jnp.zeros(rsb.shape, BF16)
    for t in range(dtiles + 1, qtiles):
        for s in range(2):
            g_send[1, t // per, s, t % per] = jnp.zeros((R, HD), BF16)

    chosen = rp_ref[0, 0]
    length = rl_ref[0, 0]
    reward = rew_ref[0, 0]
    pick = [(chosen == s).astype(F32) for s in range(2)]
    ten = [pt_ref[0], pt_ref[1]]
    own_ten = jnp.where(chosen == 0, ten[0], ten[1])

    row8 = lax.broadcasted_iota(jnp.int32, (8, HD), 0)
    stat[0] = jnp.where(
        row8 == 0,
        reward * pick[0],
        jnp.where(
            row8 == 1,
            reward * pick[1],
            jnp.where(row8 == 2, pick[0], jnp.where(row8 == 3, pick[1], 0.0)),
        ),
    )

    pl.semaphore_wait(barrier, SIDE - 1 + NZ - 1 + 1)

    def spread(buf, s, i):
        return Spread(at, buf.at[s], s, sp_send, sp_recv, i * SPREAD_SEMS)

    ko = [spread(k_own, s, s) for s in range(2)]
    kp = [spread(k_par, s, 2 + s) for s in range(2)]
    vo = [spread(v_own, s, 4 + s) for s in range(2)]
    vp = [spread(v_par, s, 6 + s) for s in range(2)]
    partner = at.line(4)[0]

    def across(src, dst, s, i):
        a, b = (at.x, at.y) if s == 0 else (at.y, at.x)
        return pltpu.make_async_remote_copy(
            src_ref=src.at[s, a, b], dst_ref=dst.at[s, a, b],
            send_sem=z_send.at[i], recv_sem=z_recv.at[i],
            device_id=partner, device_id_type=MESH,
        )

    zk = [across(k_own, k_par, s, s) for s in range(2)]
    zv = [across(v_own, v_par, s, 2 + s) for s in range(2)]
    for s in range(2):
        zk[s].start()
    for s in range(2):
        ko[s].first()

    def stat_copy(step, d):
        i = step * 3 + d - 1
        device = partner if step == 2 else at.along(step, d)
        return pltpu.make_async_remote_copy(
            src_ref=stat.at[step], dst_ref=stat_in.at[i],
            send_sem=st_send.at[i], recv_sem=st_recv.at[i],
            device_id=device, device_id_type=MESH,
        )

    stat_copies = [[stat_copy(0, d) for d in (1, 2, 3)], [stat_copy(1, d) for d in (1, 2, 3)], [stat_copy(2, 1)]]

    def stat_start(step):
        for c in stat_copies[step]:
            c.start()

    def stat_sum(step):
        total = stat[step]
        for i, c in enumerate(stat_copies[step]):
            c.wait_recv()
            total = total + stat_in[step * 3 + i]
        stat[step + 1] = total

    stat_start(0)

    loads[0].wait()
    loads[1].wait()
    for s in range(2):
        a, b = (at.x, at.y) if s == 0 else (at.y, at.x)
        low = dot_nt(vd[ten[s]], ph[s]).astype(BF16)
        v_own[s, a, b, PB : PB + R, 0:PB] = low
    for s in range(2):
        ko[s].second()
    for s in range(2):
        zv[s].start()
    for s in range(2):
        vo[s].first()

    loads[2].wait()
    loads[3].wait()
    low_qv = dot_nt(jnp.concatenate([qd[own_ten], vd[own_ten]], axis=0), rh[...]).astype(BF16)
    low_q = low_qv[0:R]
    low_v = low_qv[R : 2 * R]
    q_up = qu_ref[own_ten]
    v_up = vu_ref[own_ten]
    queries = (rq_ref[...].astype(F32) + 2.0 * dot_tn(low_q, q_up)).astype(BF16)
    own_val = (rv_ref[...].astype(F32) + 2.0 * dot_tn(low_v, v_up)).astype(BF16)
    qh = jnp.concatenate([queries[:, h * HD : (h + 1) * HD] for h in range(HQ)], axis=0)
    rk = rk_ref[...]
    stat_sum(0)
    stat_start(1)

    for s in range(2):
        zk[s].wait_recv()
        kp[s].first()
    for s in range(2):
        ko[s].relay()
    for s in range(2):
        kp[s].second()
    for s in range(2):
        vo[s].second()

    factor = HD ** (-0.5) * LOG2E
    s_own = dot_nt(qh, rk)
    q_pos = lax.rem(lax.broadcasted_iota(jnp.int32, (rows, RL), 0), RL)
    k_pos = lax.broadcasted_iota(jnp.int32, (rows, RL), 1)
    allowed = (k_pos <= q_pos) & (k_pos < length)
    m_own = jnp.max(jnp.where(allowed, s_own, -1e30), axis=1, keepdims=True)

    stat_sum(1)
    stat_start(2)
    cols = 4 * PB
    for s in range(2):
        ko[s].finish()

    def scores(kbuf, base):
        def body(a, _):
            kc = kbuf[chosen, a].reshape(cols, HD)
            sc = dot_nt(qh, kc)
            s_scr[base + a] = sc
            top = sc[:, 0:HD]
            for j in range(1, cols // HD):
                top = jnp.maximum(top, sc[:, j * HD : (j + 1) * HD])
            m_scr[...] = jnp.maximum(m_scr[...], top)
            return 0

        lax.fori_loop(0, 4, body, 0)

    m_scr[...] = jnp.broadcast_to(m_own, (rows, HD))
    scores(k_own, 0)

    for s in range(2):
        zv[s].wait_recv()
        vp[s].first()
    for s in range(2):
        kp[s].relay()
    for s in range(2):
        vo[s].relay()
    for s in range(2):
        vp[s].second()
    for s in range(2):
        kp[s].finish()
    scores(k_par, 4)

    top = jnp.max(m_scr[...], axis=1, keepdims=True) * factor
    m_scr[...] = jnp.broadcast_to(top, (rows, HD))
    l_scr[...] = jnp.zeros((rows, HD), F32)

    def exps(c, _):
        sc = s_scr[c]
        mb = m_scr[...]
        part = l_scr[...]
        for j in range(cols // HD):
            ex = jnp.exp2(sc[:, j * HD : (j + 1) * HD] * factor - mb)
            part = part + ex
            e_scr[c, :, j * HD : (j + 1) * HD] = ex.astype(BF16)
        l_scr[...] = part
        return 0

    lax.fori_loop(0, 8, exps, 0)
    e_own = jnp.where(allowed, jnp.exp2(s_own * factor - top), 0.0)
    total = jnp.sum(l_scr[...], axis=1, keepdims=True) + jnp.sum(e_own, axis=1, keepdims=True)
    inv = 1.0 / total

    stat_sum(2)
    st = stat[3]
    mean = pick[0] * st[0:1] / jnp.maximum(st[2:3], 1.0) + pick[1] * st[1:2] / jnp.maximum(st[3:4], 1.0)
    weight = -(reward - mean) / RL
    live = (lax.broadcasted_iota(jnp.int32, (RL, HD), 0) < length).astype(F32) * weight
    ct = cot_ref[...].astype(F32)
    up = jnp.concatenate(
        [(ct[:, h * HD : (h + 1) * HD] * live).astype(BF16) for h in range(HQ)], axis=0
    )
    up32 = up.astype(F32)
    un = (up32 * inv).astype(BF16)
    uv = dot_nt(v_up, un).astype(BF16)
    e_own16 = e_own.astype(BF16)

    row_r = lax.broadcasted_iota(jnp.int32, (R, HD), 0)
    col_r = lax.broadcasted_iota(jnp.int32, (R, HD), 1)
    lift = jnp.concatenate(
        [2.0 * v_up.astype(F32), (row_r == col_r).astype(F32)], axis=1
    ).astype(BF16)

    def values(vbuf, base):
        def body(a, _):
            blk = vbuf[chosen, a]
            low_t = jnp.concatenate([blk[j, PB : PB + R, :] for j in range(4)], axis=1)
            ext = dot_tn(low_t, lift)
            for j in range(4):
                v_scr[base + a, j * PB : (j + 1) * PB, 0:HD] = (
                    blk[j, 0:PB, :].astype(F32) + ext[j * HD : j * HD + PB, 0:HD]
                ).astype(BF16)
                v_scr[base + a, j * PB : (j + 1) * PB, HD : 2 * HD] = ext[
                    j * HD : j * HD + PB, HD : 2 * HD
                ].astype(BF16)
            o_scr[...] += dot_nn(e_scr[base + a], v_scr[base + a])
            return 0

        lax.fori_loop(0, 4, body, 0)

    o_scr[:, 0:HD] = dot_nn(e_own16, own_val)
    o_scr[:, HD : 2 * HD] = jnp.zeros((rows, HD), F32)
    for s in range(2):
        vo[s].finish()
    values(v_own, 0)
    for s in range(2):
        vp[s].relay()
    for s in range(2):
        vp[s].finish()
    values(v_par, 4)

    attended = o_scr[:, 0:HD] * inv
    for h in range(HQ):
        attn_ref[:, h * HD : (h + 1) * HD] = attended[h * RL : (h + 1) * RL].astype(BF16)
    delta = jnp.sum(up32 * attended, axis=1, keepdims=True) * inv
    wl = o_scr[:, HD : HD + R].astype(BF16)
    vup_term = 2.0 * dot_tn(wl, un)

    ds_own = (e_own * (dot_nt(un, own_val) - delta)).astype(BF16)
    dq_scr[...] = dot_nn(ds_own, rk)
    m_scr[...] = jnp.broadcast_to(delta, (rows, HD))

    def backward(kbuf, base, z):
        def body(a, _):
            e16 = e_scr[base + a]
            dp = dot_nt(un, v_scr[base + a, :, 0:HD])
            db = m_scr[...]
            ds = jnp.concatenate(
                [
                    (
                        e16[:, j * HD : (j + 1) * HD].astype(F32)
                        * (dp[:, j * HD : (j + 1) * HD] - db)
                    ).astype(BF16)
                    for j in range(cols // HD)
                ],
                axis=1,
            )
            kc = kbuf[chosen, a].reshape(cols, HD)
            dq_scr[...] += dot_nn(ds, kc)
            back = dot_nn(uv, e16)
            for j in range(4):
                piece = back[:, j * PB : (j + 1) * PB]
                rsb[a * 4 + j, z, 0, :, 0:PB] = (piece * pick[0]).astype(BF16)
                rsb[j * 4 + a, z, 1, :, 0:PB] = (piece * pick[1]).astype(BF16)
            return 0

        lax.fori_loop(0, 4, body, 0)

    backward(k_own, 0, at.zh)
    backward(k_par, 4, 1 - at.zh)

    def plane_copy(src, dst, send, recv, k):
        device, p = at.plane(k // 4, lax.rem(k, 4))
        return pltpu.make_async_remote_copy(
            src_ref=src.at[p], dst_ref=dst.at[k], send_sem=send.at[k], recv_sem=recv.at[k],
            device_id=device, device_id_type=MESH,
        )

    def plane_start(src, dst, send, recv):
        def body(k, _):
            plane_copy(src, dst, send, recv, k).start()
            return 0

        lax.fori_loop(1, SIDE, body, 0)

    def plane_sum(src, dst, send, recv):
        def body(k, total):
            plane_copy(src, dst, send, recv, k).wait_recv()
            return total + dst[k].astype(F32)

        return lax.fori_loop(1, SIDE, body, src[at.p].astype(F32))

    def plane_drain(src, dst, send, recv):
        def body(k, _):
            plane_copy(src, dst, send, recv, k).wait_send()
            return 0

        lax.fori_loop(1, SIDE, body, 0)

    back_set = (rsb, rsr, rs_send, rs_recv)
    grad_set = [(g_send.at[i], g_in.at[i], g_ssem.at[i], g_rsem.at[i]) for i in range(2)]
    plane_start(*back_set)

    dq = (dq_scr[...] * (HD ** (-0.5))).astype(BF16)
    dq_wide = jnp.concatenate([dq[h * RL : (h + 1) * RL] for h in range(HQ)], axis=1)
    dov = dot_tn(e_own16, un).astype(BF16)
    qb = dot_nt(q_up, dq_wide).astype(BF16)
    vb = dot_nt(v_up, dov).astype(BF16)
    down = 2.0 * dot_nn(jnp.concatenate([qb, vb], axis=0), rh[...])
    q_term_up = 2.0 * dot_nn(low_q, dq_wide)
    vup_term = vup_term + 2.0 * dot_nn(low_v, dov)
    for t in range(qtiles):
        if t < dtiles:
            tile = down[0:R, t * HD : (t + 1) * HD]
        else:
            tile = q_term_up[:, (t - dtiles) * HD : (t - dtiles + 1) * HD]
        for s in range(2):
            g_send[0, t // per, s, t % per] = (tile * pick[s]).astype(BF16)
    vterm[...] = down[R : 2 * R]
    for s in range(2):
        g_send[1, dtiles // per, s, dtiles % per] = (vup_term * pick[s]).astype(BF16)
    plane_start(*grad_set[0])

    total_back = plane_sum(*back_set)
    bs32[...] = total_back
    bs16[...] = total_back.astype(BF16)
    bz = pltpu.make_async_remote_copy(
        src_ref=bs16.at[1 - at.zh], dst_ref=bz_in, send_sem=bz_sem.at[0], recv_sem=bz_sem.at[1],
        device_id=partner, device_id_type=MESH,
    )
    bz.start()

    r16 = lax.broadcasted_iota(jnp.int32, (R, HD), 0)
    owner = jnp.where(r16 < T, ten[0], ten[1])
    mask = (owner == lax.rem(r16, T)).astype(F32).astype(BF16)

    def line_copy(i, k, sender):
        device, _ = at.line(k)
        spot = zbuf.at[i, sender]
        return pltpu.make_async_remote_copy(
            src_ref=spot, dst_ref=spot, send_sem=zl_ssem.at[i, k], recv_sem=zl_rsem.at[i, k],
            device_id=device, device_id_type=MESH,
        )

    def line_start(i):
        total = plane_sum(*grad_set[i]).astype(BF16)
        zbuf[i, at.z, 0 : 2 * per] = total.reshape(2 * per, R, HD)
        zbuf[i, at.z, 2 * per] = mask

        def body(k, _):
            line_copy(i, k, at.z).start()
            return 0

        lax.fori_loop(1, NZ, body, 0)

    def core_copy(i):
        return pltpu.make_async_remote_copy(
            src_ref=acc16.at[i, 1 - at.c], dst_ref=core_in.at[i], send_sem=c_sem.at[i, 0],
            recv_sem=c_sem.at[i, 1], device_id=at.other_core(), device_id_type=MESH,
        )

    def line_sum(i):
        def waits(k, _):
            line_copy(i, k, lax.rem(at.z + NZ - k, NZ)).wait_recv()
            return 0

        lax.fori_loop(1, NZ, waits, 0)
        acc32[i] = jnp.zeros(acc32.shape[1:], F32)

        def body(z, _):
            tag = zbuf[i, z, 2 * per].astype(F32)
            for s in range(2):
                data = zbuf[i, z, s * per : (s + 1) * per].astype(F32)
                for t in range(T):
                    part = data * tag[s * T + t : s * T + t + 1][None]
                    acc32[i, t // half_t, t % half_t] += part
            return 0

        lax.fori_loop(0, NZ, body, 0)
        acc16[i] = acc32[i].astype(BF16)
        core_copy(i).start()

    streams = [
        [
            Spread(
                at, gath.at[i, at.c, h], h, sp_send, sp_recv, (8 + i * 2 + h) * SPREAD_SEMS
            )
            for h in range(2)
        ]
        for i in range(2)
    ]

    def gather_start(i):
        core_copy(i).wait_recv()
        final = (acc32[i, at.c] + core_in[i].astype(F32)).astype(BF16)
        for h in range(2):
            a, b = (at.x, at.y) if h == 0 else (at.y, at.x)
            gath[i, at.c, h, a, b] = final[2 * h : 2 * h + 2]
            streams[i][h].first()

    def final_copy(i, h, core):
        spot = gath.at[i, core, h]
        return pltpu.make_async_remote_copy(
            src_ref=spot, dst_ref=spot, send_sem=f_sem.at[i, h, 0], recv_sem=f_sem.at[i, h, 1],
            device_id=at.other_core(), device_id_type=MESH,
        )

    def gather_second(i):
        for h in range(2):
            streams[i][h].second()

    def gather_relay(i):
        for h in range(2):
            streams[i][h].relay()

    def gather_finish(i):
        for h in range(2):
            streams[i][h].finish()
            final_copy(i, h, at.c).start()

    line_start(0)

    bz.wait_recv()
    back = (bs32[at.zh] + bz_in[...].astype(F32)).astype(BF16)
    for s in range(2):
        term = 2.0 * dot_nn(back[s][:, 0:PB], ph[s]) + vterm[...] * pick[s]
        for t in range(dtiles):
            g_send[1, t // per, s, t % per] = term[:, t * HD : (t + 1) * HD].astype(BF16)
    plane_start(*grad_set[1])

    line_sum(0)
    gather_start(0)
    gather_second(0)
    line_start(1)
    gather_relay(0)
    line_sum(1)
    gather_start(1)
    gather_finish(0)
    gather_second(1)
    gather_relay(1)
    gather_finish(1)

    for c in zk + zv + [bz] + [c for step in stat_copies for c in step]:
        c.wait_send()
    for g in ko + kp + vo + vp + streams[0] + streams[1]:
        g.drain()
    plane_drain(*back_set)
    for i in range(2):
        plane_drain(*grad_set[i])

        def body(k, _):
            line_copy(i, k, at.z).wait_send()
            return 0

        lax.fori_loop(1, NZ, body, 0)
        core_copy(i).wait_send()
        for h in range(2):
            final_copy(i, h, at.c).wait_send()
            final_copy(i, h, 1 - at.c).wait_recv()


def widen_kernel(dims, gath, qd_ref, qu_ref, vd_ref, vu_ref):
    (D, HD, HQ, R, T, PB, RL) = dims
    t = pl.program_id(0)
    h = lax.rem(t, 4) // 2
    qtiles = (D + HQ * HD) // HD
    dtiles = D // HD
    per = qtiles // SIDE
    for i in range(2):
        for k in range(qtiles):
            p, j = k // per, k % per
            x, y = p // 4, p % 4
            a = jnp.where(h == 0, x, y)
            b = jnp.where(h == 0, y, x)
            if i == 1 and k > dtiles:
                continue
            tile = gath[i, 0, 0, a, b, 0, j].astype(F32)
            if k < dtiles:
                ref = qd_ref if i == 0 else vd_ref
                ref[0, :, k * HD : (k + 1) * HD] = tile
            else:
                ref = qu_ref if i == 0 else vu_ref
                ref[0, :, (k - dtiles) * HD : (k - dtiles + 1) * HD] = tile


def per_device(
    prompt_hidden, prompt_keys, prompt_values, resp_hidden, resp_queries, resp_keys, resp_values,
    cotangent, rewards, resp_prompt, resp_len, prompt_tenant, q_down, q_up, v_down, v_up,
):
    D = prompt_hidden.shape[2]
    PB = prompt_hidden.shape[1]
    HD = prompt_keys.shape[2]
    HQ = resp_queries.shape[2] // HD
    T, _, R = q_down.shape
    RL = resp_hidden.shape[1]
    dims = (D, HD, HQ, R, T, PB, RL)
    rows = RL * HQ
    per = (D + HQ * HD) // HD // SIDE
    cols = 4 * PB
    vmem = pl.BlockSpec(memory_space=pltpu.VMEM)
    smem = pl.BlockSpec(memory_space=pltpu.SMEM)
    hbm = pl.BlockSpec(memory_space=pl.ANY)
    dma = pltpu.SemaphoreType.DMA
    gath_shape = (2, 2, 2, 4, 4, 2, per, R, HD)
    attn, gath = pl.pallas_call(
        functools.partial(step_kernel, dims),
        name="step",
        out_shape=(
            jax.ShapeDtypeStruct((RL, HQ * HD), BF16),
            jax.ShapeDtypeStruct(gath_shape, BF16),
        ),
        in_specs=[hbm, vmem, vmem, hbm, vmem, vmem, vmem, vmem, smem, smem, smem, smem, hbm, vmem, hbm, vmem],
        out_specs=(vmem, vmem),
        scratch_shapes=[
            pltpu.VMEM((2, PB, D), BF16),
            pltpu.VMEM((RL, D), BF16),
            pltpu.VMEM((T, R, D), BF16),
            pltpu.VMEM((T, R, D), BF16),
            pltpu.VMEM((2, 4, 4, PB, HD), BF16),
            pltpu.VMEM((2, 4, 4, PB, HD), BF16),
            pltpu.VMEM((2, 4, 4, PB + R, HD), BF16),
            pltpu.VMEM((2, 4, 4, PB + R, HD), BF16),
            pltpu.VMEM((8, rows, cols), F32),
            pltpu.VMEM((8, rows, cols), BF16),
            pltpu.VMEM((8, cols, 2 * HD), BF16),
            pltpu.VMEM((rows, HD), F32),
            pltpu.VMEM((rows, HD), F32),
            pltpu.VMEM((rows, 2 * HD), F32),
            pltpu.VMEM((rows, HD), F32),
            pltpu.VMEM((4, 8, HD), F32),
            pltpu.VMEM((7, 8, HD), F32),
            pltpu.VMEM((SIDE, 2, 2, R, HD), BF16),
            pltpu.VMEM((SIDE, 2, 2, R, HD), BF16),
            pltpu.VMEM((2, 2, R, HD), F32),
            pltpu.VMEM((2, 2, R, HD), BF16),
            pltpu.VMEM((2, R, HD), BF16),
            pltpu.VMEM((2, SIDE, 2, per, R, HD), BF16),
            pltpu.VMEM((2, SIDE, 2, per, R, HD), BF16),
            pltpu.VMEM((2, NZ, 2 * per + 1, R, HD), BF16),
            pltpu.VMEM((2, 2, T // 2, per, R, HD), F32),
            pltpu.VMEM((2, 2, T // 2, per, R, HD), BF16),
            pltpu.VMEM((2, T // 2, per, R, HD), BF16),
            pltpu.VMEM((R, D), F32),
            dma((4,)),
            dma((12 * SPREAD_SEMS,)),
            dma((12 * SPREAD_SEMS,)),
            dma((4,)),
            dma((4,)),
            dma((7,)),
            dma((7,)),
            dma((SIDE,)),
            dma((SIDE,)),
            dma((2,)),
            dma((2, SIDE)),
            dma((2, SIDE)),
            dma((2, NZ)),
            dma((2, NZ)),
            dma((2, 2)),
            dma((2, 2, 2)),
        ],
        compiler_params=pltpu.CompilerParams(
            collective_id=0, has_side_effects=True, vmem_limit_bytes=56 * 2**20
        ),
    )(
        prompt_hidden, prompt_keys, prompt_values, resp_hidden[0], resp_queries[0], resp_keys[0],
        resp_values[0], cotangent[0], rewards, resp_prompt, resp_len, prompt_tenant,
        jnp.swapaxes(q_down, 1, 2), q_up, jnp.swapaxes(v_down, 1, 2), v_up,
    )

    def out_block(width):
        return pl.BlockSpec((1, R, width), lambda t: (t, 0, 0))

    qd_t, g_qu, vd_t, g_vu = pl.pallas_call(
        functools.partial(widen_kernel, dims),
        name="widen",
        grid=(T,),
        out_shape=(
            jax.ShapeDtypeStruct((T, R, D), F32),
            jax.ShapeDtypeStruct((T, R, HQ * HD), F32),
            jax.ShapeDtypeStruct((T, R, D), F32),
            jax.ShapeDtypeStruct((T, R, HD), F32),
        ),
        in_specs=[
            pl.BlockSpec(
                (2, 1, 1, 4, 4, 1, per, R, HD),
                lambda t: (0, t // 4, lax.rem(t, 4) // 2, 0, 0, lax.rem(t, 2), 0, 0, 0),
            )
        ],
        out_specs=(out_block(D), out_block(HQ * HD), out_block(D), out_block(HD)),
    )(gath)
    return (
        attn[None],
        jnp.swapaxes(qd_t, 1, 2),
        g_qu,
        jnp.swapaxes(vd_t, 1, 2),
        g_vu,
    )


def solution(mesh):
    rows = P("prompt", "resp", None)
    pair = P("prompt", "resp")
    return jax.shard_map(
        per_device,
        mesh=mesh,
        in_specs=(rows,) * 8 + (pair,) * 3 + (P("prompt"),) + (P(),) * 4,
        out_specs=(rows, P(), P(), P(), P()),
        check_vma=False,
    )
```

```python
import functools

import jax
import jax.numpy as jnp
from jax import lax
from jax.experimental import pallas as pl
from jax.experimental.pallas import tpu as pltpu
from jax.sharding import PartitionSpec as P

MESH = pl.DeviceIdType.MESH
F32 = jnp.float32
BF16 = jnp.bfloat16
NX = 4
NZ = 8
SIDE = NX * NX
LOG2E = 1.4426950408889634


def dot_nn(a, b):
    return lax.dot_general(a, b, (((1,), (0,)), ((), ())), preferred_element_type=F32)


def dot_nt(a, b):
    return lax.dot_general(a, b, (((1,), (1,)), ((), ())), preferred_element_type=F32)


def dot_tn(a, b):
    return lax.dot_general(a, b, (((0,), (0,)), ((), ())), preferred_element_type=F32)


class Place:
    def __init__(self):
        r = lax.axis_index("resp")
        p = lax.axis_index("prompt")
        self.x = r // 8
        self.y = lax.rem(r // 2, 4)
        self.zh = lax.rem(r, 2)
        self.zl = p // 2
        self.c = lax.rem(p, 2)
        self.z = self.zh * 4 + self.zl
        self.p = self.x * 4 + self.y

    def plane(self, dx, dy):
        x = lax.rem(self.x + dx, 4)
        y = lax.rem(self.y + dy, 4)
        return {"resp": (x * 4 + y) * 2 + self.zh}, x * 4 + y

    def line(self, dz):
        z = lax.rem(self.z + dz, NZ)
        return {
            "prompt": lax.rem(z, 4) * 2 + self.c,
            "resp": self.p * 2 + z // 4,
        }, z

    def other_core(self):
        return {"prompt": self.zl * 2 + (1 - self.c)}

    def along(self, axis, d):
        return self.plane(d, 0)[0] if axis == 0 else self.plane(0, d)[0]


class Spread:
    def __init__(self, at, buf, axis, send, recv, base, forward=None):
        self.at = at
        self.buf = buf
        self.axis = axis
        self.a = at.x if axis == 0 else at.y
        self.b = at.y if axis == 0 else at.x
        self.send = send
        self.recv = recv
        self.base = base
        self.sent = []
        self.forward = forward or (lambda ref, step: None)

    def copy(self, src, dst, sem, device):
        return pltpu.make_async_remote_copy(
            src_ref=src,
            dst_ref=dst,
            send_sem=self.send.at[self.base + sem],
            recv_sem=self.recv.at[self.base + sem],
            device_id=device,
            device_id_type=MESH,
        )

    def push(self, ref, sem, device):
        c = self.copy(ref, ref, sem, device)
        c.start()
        self.sent.append(c)

    def take(self, ref, sem, device):
        self.copy(ref, ref, sem, device).wait_recv()

    def first(self):
        mine = self.buf.at[self.a, self.b]
        for d in (1, 3, 2):
            self.push(mine, d - 1, self.at.along(1 - self.axis, d))

    def second(self):
        for d in (1, 3, 2):
            self.take(
                self.buf.at[self.a, lax.rem(self.b + 4 - d, 4)],
                d - 1,
                self.at.along(1 - self.axis, d),
            )
        row = self.buf.at[self.a]
        self.push(row, 3, self.at.along(self.axis, 1))
        self.push(row, 4, self.at.along(self.axis, 3))
        self.forward(row, 0)

    def relay(self):
        low = lax.rem(self.a + 3, 4)
        high = lax.rem(self.a + 1, 4)
        self.take(self.buf.at[low], 3, self.at.along(self.axis, 1))
        self.push(self.buf.at[low, pl.ds(0, 2)], 5, self.at.along(self.axis, 1))
        self.forward(self.buf.at[low], 1)
        self.take(self.buf.at[high], 4, self.at.along(self.axis, 3))
        self.push(self.buf.at[high, pl.ds(2, 2)], 6, self.at.along(self.axis, 3))
        self.forward(self.buf.at[high], 2)

    def finish(self):
        far = lax.rem(self.a + 2, 4)
        self.take(self.buf.at[far, pl.ds(0, 2)], 5, self.at.along(self.axis, 1))
        self.take(self.buf.at[far, pl.ds(2, 2)], 6, self.at.along(self.axis, 3))
        self.forward(self.buf.at[far], 3)

    def drain(self):
        for c in self.sent:
            c.wait_send()


SPREAD_SEMS = 7
HOLD_SEMS = 9


class Hold:
    def __init__(self, at, raw, sel, out, send, recv, base):
        self.at = at
        self.raw = raw
        self.sel = sel
        self.out = out
        self.send = send
        self.recv = recv
        self.base = base
        self.par = lax.rem(at.x + at.y, 2)
        self.sent = []

    def copy(self, src, dst, sem, device):
        return pltpu.make_async_remote_copy(
            src_ref=src,
            dst_ref=dst,
            send_sem=self.send.at[self.base + sem],
            recv_sem=self.recv.at[self.base + sem],
            device_id=device,
            device_id_type=MESH,
        )

    def spot(self, par, x, y):
        return par, par * (x // 2) + (1 - par) * (y // 2)

    def mine(self):
        return self.raw.at[self.spot(self.par, self.at.x, self.at.y)]

    def columns(self, x):
        return self.out.at[lax.rem(x, 2), x // 2, lax.rem(x, 2)]

    def rows(self, y):
        return self.out.at[1 - lax.rem(y, 2), :, lax.rem(y, 2), y // 2]

    def first(self):
        mine = self.mine()
        for d in (1, 3, 2):
            c = self.copy(mine, mine, d - 1, self.at.plane(d * self.par, d * (1 - self.par))[0])
            c.start()
            self.sent.append(c)

    def second(self, picks, own):
        at = self.at
        for d in (1, 3, 2):
            par = lax.rem(self.par + d, 2)
            x = lax.rem(at.x + (4 - d) * par, 4)
            y = lax.rem(at.y + (4 - d) * (1 - par), 4)
            spot = self.raw.at[self.spot(par, x, y)]
            self.copy(spot, spot, d - 1, at.along(0, d)).wait_recv()
        for d in (1, 3, 2):
            for axis in range(2):
                p = picks(axis, d)
                self.sel[axis, d - 1] = self.raw[axis, :, 0] * p[0] + self.raw[axis, :, 1] * p[1]
                target = self.columns(at.x) if axis == 0 else self.rows(at.y)
                c = self.copy(self.sel.at[axis, d - 1], target, 3 + axis * 3 + d - 1, at.along(axis, d))
                c.start()
                self.sent.append(c)
        chosen = [self.raw[axis, :, 0] * own[0] + self.raw[axis, :, 1] * own[1] for axis in range(2)]
        self.out[lax.rem(at.x, 2), at.x // 2, lax.rem(at.x, 2)] = chosen[0]
        for i in range(2):
            self.out[1 - lax.rem(at.y, 2), i, lax.rem(at.y, 2), at.y // 2] = chosen[1][i]

    def finish(self):
        at = self.at
        for d in (1, 3, 2):
            spot = self.columns(lax.rem(at.x + 4 - d, 4))
            self.copy(spot, spot, 3 + d - 1, at.along(0, d)).wait_recv()
            spot = self.rows(lax.rem(at.y + 4 - d, 4))
            self.copy(spot, spot, 6 + d - 1, at.along(1, d)).wait_recv()

    def drain(self):
        for c in self.sent:
            c.wait_send()


def step_kernel(
    dims,
    ph_hbm, pk_hbm, pv_hbm, rh_hbm, rq_hbm, rk_hbm, rv_hbm, cot_hbm,
    rew_ref, rp_ref, rl_ref, pt_ref, qd_hbm, qu_hbm, vd_hbm, vu_hbm,
    attn_ref, gath_hbm,
    gath, ph, rh, qd, vd, rq_ref, rk_ref, rv_ref, cot_ref, qu_ref, vu_ref,
    k_raw, v_raw, k_sel, v_sel, k_all, v_all,
    s_scr, e_scr, v_scr, m_scr, l_scr, o_scr, dq_scr,
    stat, stat_in,
    rsb, rsr, bs32, bs16, bz_in,
    g_send, g_in, zbuf, tags, acc32, acc16, core_in, vterm,
    load_sem, h_send, h_recv, sp_send, sp_recv, z_send, z_recv, st_send, st_recv,
    rs_send, rs_recv, bz_sem, g_ssem, g_rsem, zl_ssem, zl_rsem, tag_ssem, tag_rsem, c_sem, f_sem, out_sem,
):
    (D, HD, HQ, R, T, PB, RL) = dims
    at = Place()
    rows = RL * HQ
    qtiles = (D + HQ * HD) // HD
    dtiles = D // HD
    per = qtiles // SIDE
    half_t = T // 2

    barrier = pltpu.get_barrier_semaphore()

    def greet_plane(k, _):
        pl.semaphore_signal(
            barrier, inc=1, device_id=at.plane(k // 4, lax.rem(k, 4))[0], device_id_type=MESH
        )
        return 0

    def greet_line(k, _):
        pl.semaphore_signal(barrier, inc=1, device_id=at.line(k)[0], device_id_type=MESH)
        return 0

    lax.fori_loop(1, SIDE, greet_plane, 0)
    lax.fori_loop(1, NZ, greet_line, 0)
    pl.semaphore_signal(barrier, inc=1, device_id=at.other_core(), device_id_type=MESH)

    par = lax.rem(at.x + at.y, 2)
    place = par * (at.x // 2) + (1 - par) * (at.y // 2)
    loads = [
        pltpu.make_async_copy(s, d, load_sem.at[i])
        for i, (s, d) in enumerate(
            (
                (pk_hbm, k_raw.at[0, par, place]),
                (pv_hbm, v_raw.at[0, par, place, :, pl.ds(0, PB)]),
                (ph_hbm, ph),
                (vd_hbm, vd),
                (rh_hbm, rh),
                (qd_hbm, qd),
                (rq_hbm, rq_ref),
                (qu_hbm, qu_ref),
                (vu_hbm, vu_ref),
                (rk_hbm, rk_ref),
                (rv_hbm, rv_ref),
                (cot_hbm, cot_ref),
            )
        )
    ]
    for c in loads:
        c.start()

    for s in range(2):
        v_raw[0, par, place, s, PB : PB + R, :] = jnp.zeros((R, HD), BF16)
    rsb[...] = jnp.zeros(rsb.shape, BF16)
    for t in range(dtiles + 1, qtiles):
        for s in range(2):
            g_send[1, t // per, s, t % per] = jnp.zeros((R, HD), BF16)

    chosen = rp_ref[0, 0]
    length = rl_ref[0, 0]
    reward = rew_ref[0, 0]
    pick = [(chosen == s).astype(F32) for s in range(2)]
    ten = [pt_ref[0], pt_ref[1]]
    own_ten = jnp.where(chosen == 0, ten[0], ten[1])

    row8 = lax.broadcasted_iota(jnp.int32, (8, HD), 0)
    stat[0] = jnp.where(
        row8 == 0,
        reward * pick[0],
        jnp.where(
            row8 == 1,
            reward * pick[1],
            jnp.where(row8 == 2, pick[0], jnp.where(row8 == 3, pick[1], 0.0)),
        ),
    )

    loads[0].wait()
    pl.semaphore_wait(barrier, SIDE - 1 + NZ - 1 + 1)

    def hold(raw, sel, out, z, i):
        return Hold(at, raw.at[z], sel.at[z], out.at[z], h_send, h_recv, i * HOLD_SEMS)

    ko, kp = [hold(k_raw, k_sel, k_all, z, z) for z in range(2)]
    vo, vp = [hold(v_raw, v_sel, v_all, z, 2 + z) for z in range(2)]
    partner = at.line(4)[0]

    def across(raw, i):
        return pltpu.make_async_remote_copy(
            src_ref=raw.at[0, par, place], dst_ref=raw.at[1, par, place],
            send_sem=z_send.at[i], recv_sem=z_recv.at[i],
            device_id=partner, device_id_type=MESH,
        )

    zk = across(k_raw, 0)
    zv = across(v_raw, 1)
    zk.start()
    ko.first()

    def stat_copy(step, d):
        i = step * 3 + d - 1
        device = partner if step == 2 else at.along(step, d)
        return pltpu.make_async_remote_copy(
            src_ref=stat.at[step], dst_ref=stat_in.at[i],
            send_sem=st_send.at[i], recv_sem=st_recv.at[i],
            device_id=device, device_id_type=MESH,
        )

    def pick_copy(d):
        return pltpu.make_async_remote_copy(
            src_ref=stat.at[0], dst_ref=stat_in.at[6 + d],
            send_sem=st_send.at[6 + d], recv_sem=st_recv.at[6 + d],
            device_id=at.along(1, d), device_id_type=MESH,
        )

    stat_copies = [[stat_copy(0, d) for d in (1, 2, 3)], [stat_copy(1, d) for d in (1, 2, 3)], [stat_copy(2, 1)]]
    pick_copies = [pick_copy(d) for d in (1, 2, 3)]

    def stat_start(step):
        for c in stat_copies[step]:
            c.start()

    def stat_sum(step):
        total = stat[step]
        for i, c in enumerate(stat_copies[step]):
            c.wait_recv()
            total = total + stat_in[step * 3 + i]
        stat[step + 1] = total

    def picks(axis, d):
        tile = stat_in[(0 if axis == 0 else 7) + 3 - d].astype(BF16)
        return [tile[2 + s : 3 + s] for s in range(2)]

    own_pick = [stat[0].astype(BF16)[2 + s : 3 + s] for s in range(2)]

    stat_start(0)
    for c in pick_copies:
        c.start()
    for i in (1, 2, 3):
        loads[i].wait()
    for s in range(2):
        low = dot_nt(vd[ten[s]], ph[s]).astype(BF16)
        v_raw[0, par, place, s, PB : PB + R, 0:PB] = low

    vo.first()

    r16 = lax.broadcasted_iota(jnp.int32, (R, HD), 0)
    owner = jnp.where(r16 < T, ten[0], ten[1])
    mask = (owner == lax.rem(r16, T)).astype(F32).astype(BF16)

    tags[at.z] = mask

    def tag_copy(k, sender):
        spot = tags.at[sender]
        return pltpu.make_async_remote_copy(
            src_ref=spot, dst_ref=spot, send_sem=tag_ssem.at[k], recv_sem=tag_rsem.at[k],
            device_id=at.line(k)[0], device_id_type=MESH,
        )

    def tag_start(k, _):
        tag_copy(k, at.z).start()
        return 0

    def tag_wait(k, _):
        tag_copy(k, at.z).wait_send()
        tag_copy(k, lax.rem(at.z + NZ - k, NZ)).wait_recv()
        return 0

    for c in loads[4:]:
        c.wait()
    low_qv = dot_nt(jnp.concatenate([qd[own_ten], vd[own_ten]], axis=0), rh[...]).astype(BF16)
    low_q = low_qv[0:R]
    low_v = low_qv[R : 2 * R]
    q_up = qu_ref[own_ten]
    v_up = vu_ref[own_ten]
    queries = (rq_ref[...].astype(F32) + 2.0 * dot_tn(low_q, q_up)).astype(BF16)
    own_val = (rv_ref[...].astype(F32) + 2.0 * dot_tn(low_v, v_up)).astype(BF16)
    qh = jnp.concatenate([queries[:, h * HD : (h + 1) * HD] for h in range(HQ)], axis=0)
    rk = rk_ref[...]
    stat_sum(0)
    for c in pick_copies:
        c.wait_recv()
    ko.second(picks, own_pick)
    stat_start(1)
    vo.second(picks, own_pick)

    factor = HD ** (-0.5) * LOG2E
    s_own = dot_nt(qh, rk)
    q_pos = lax.rem(lax.broadcasted_iota(jnp.int32, (rows, RL), 0), RL)
    k_pos = lax.broadcasted_iota(jnp.int32, (rows, RL), 1)
    allowed = (k_pos <= q_pos) & (k_pos < length)
    m_own = jnp.max(jnp.where(allowed, s_own, -1e30), axis=1, keepdims=True)

    zk.wait_recv()
    kp.first()
    zv.start()
    lax.fori_loop(1, NZ, tag_start, 0)
    stat_sum(1)
    stat_start(2)
    ko.finish()

    cols = 4 * PB
    row_r = lax.broadcasted_iota(jnp.int32, (R, HD), 0)
    col_r = lax.broadcasted_iota(jnp.int32, (R, HD), 1)
    lift = jnp.concatenate(
        [2.0 * v_up.astype(F32), (row_r == col_r).astype(F32)], axis=1
    ).astype(BF16)

    def keys(c):
        return k_all[c // 4, (c % 4) // 2, c % 2].reshape(cols, HD)

    def low_rows(c):
        return jnp.concatenate(
            [v_all[c // 4, (c % 4) // 2, c % 2, j // 2, j % 2, PB : PB + R, :] for j in range(4)], axis=1
        )

    def scores(half, start):
        m_scr[...] = jnp.broadcast_to(start, (rows, HD))
        for c in range(4 * half, 4 * half + 4):
            sc = dot_nt(qh, keys(c))
            s_scr[c] = sc
            top = sc[:, 0:HD]
            for j in range(1, cols // HD):
                top = jnp.maximum(top, sc[:, j * HD : (j + 1) * HD])
            m_scr[...] = jnp.maximum(m_scr[...], top)
        top = jnp.max(m_scr[...], axis=1, keepdims=True) * factor
        m_scr[...] = jnp.broadcast_to(top, (rows, HD))
        return top

    def exps(half):
        l_scr[...] = jnp.zeros((rows, HD), F32)
        for c in range(4 * half, 4 * half + 4):
            sc = s_scr[c]
            mb = m_scr[...]
            part = l_scr[...]
            for j in range(cols // HD):
                ex = jnp.exp2(sc[:, j * HD : (j + 1) * HD] * factor - mb)
                part = part + ex
                e_scr[c, :, j * HD : (j + 1) * HD] = ex.astype(BF16)
            l_scr[...] = part
        return jnp.sum(l_scr[...], axis=1, keepdims=True)

    def values(half):
        for c in range(4 * half, 4 * half + 4):
            ext = dot_tn(low_rows(c), lift)
            blk = v_all[c // 4, (c % 4) // 2, c % 2, :, :, 0:PB, :].reshape(4, PB, HD)
            for j in range(4):
                v_scr[c, j * PB : (j + 1) * PB, 0:HD] = (
                    blk[j].astype(F32) + ext[j * HD : j * HD + PB, 0:HD]
                ).astype(BF16)
                v_scr[c, j * PB : (j + 1) * PB, HD : 2 * HD] = ext[
                    j * HD : j * HD + PB, HD : 2 * HD
                ].astype(BF16)
            o_scr[half] += dot_nn(e_scr[c], v_scr[c])

    top0 = scores(0, m_own)
    kp.second(picks, own_pick)
    l0 = exps(0)
    e_own = jnp.where(allowed, jnp.exp2(s_own * factor - top0), 0.0)
    e_own16 = e_own.astype(BF16)
    l0 = l0 + jnp.sum(e_own, axis=1, keepdims=True)
    zv.wait_recv()
    vp.first()
    o_scr[0, :, 0:HD] = dot_nn(e_own16, own_val)
    o_scr[0, :, HD : 2 * HD] = jnp.zeros((rows, HD), F32)
    o_scr[1] = jnp.zeros((rows, 2 * HD), F32)
    vo.finish()
    values(0)

    stat_sum(2)
    st = stat[3]
    mean = pick[0] * st[0:1] / jnp.maximum(st[2:3], 1.0) + pick[1] * st[1:2] / jnp.maximum(st[3:4], 1.0)
    weight = -(reward - mean) / RL
    live = (lax.broadcasted_iota(jnp.int32, (RL, HD), 0) < length).astype(F32) * weight
    ct = cot_ref[...].astype(F32)
    up = jnp.concatenate(
        [(ct[:, h * HD : (h + 1) * HD] * live).astype(BF16) for h in range(HQ)], axis=0
    )
    up32 = up.astype(F32)

    kp.finish()
    top1 = scores(1, jnp.full((rows, 1), -1e30, F32))
    vp.second(picks, own_pick)
    l1 = exps(1)
    top = jnp.maximum(top0, top1)
    share0 = jnp.exp2(top0 - top)
    share1 = jnp.exp2(top1 - top)
    inv = 1.0 / (share0 * l0 + share1 * l1)
    scale = [share0 * inv, share1 * inv]
    un = [(up32 * scale[h]).astype(BF16) for h in range(2)]

    for c in range(8):
        half = c // 4
        if c % 4 == 0:
            uv = dot_nt(v_up, un[half]).astype(BF16)
        x = (c % 2) * 2 + (c % 4) // 2
        back = dot_nn(uv, e_scr[c])
        z = at.zh if half == 0 else 1 - at.zh
        for j in range(4):
            y = (j % 2) * 2 + j // 2
            piece = back[:, j * PB : (j + 1) * PB]
            for s in range(2):
                rsb[x * 4 + y, z, s, :, 0:PB] = (piece * pick[s]).astype(BF16)

    def plane_copy(src, dst, send, recv, k):
        device, p = at.plane(k // 4, lax.rem(k, 4))
        return pltpu.make_async_remote_copy(
            src_ref=src.at[p], dst_ref=dst.at[k], send_sem=send.at[k], recv_sem=recv.at[k],
            device_id=device, device_id_type=MESH,
        )

    def plane_start(src, dst, send, recv):
        def body(k, _):
            plane_copy(src, dst, send, recv, k).start()
            return 0

        lax.fori_loop(1, SIDE, body, 0)

    def plane_sum(src, dst, send, recv):
        def body(k, total):
            plane_copy(src, dst, send, recv, k).wait_recv()
            return total + dst[k].astype(F32)

        return lax.fori_loop(1, SIDE, body, src[at.p].astype(F32))

    def plane_drain(src, dst, send, recv):
        def body(k, _):
            plane_copy(src, dst, send, recv, k).wait_send()
            return 0

        lax.fori_loop(1, SIDE, body, 0)

    back_set = (rsb, rsr, rs_send, rs_recv)
    grad_set = [(g_send.at[i], g_in.at[i], g_ssem.at[i], g_rsem.at[i]) for i in range(2)]
    plane_start(*back_set)

    dov = dot_tn(e_own16, un[0]).astype(BF16)
    vb = dot_nt(v_up, dov).astype(BF16)
    vterm[...] = 2.0 * dot_nn(vb, rh[...])
    total_back = plane_sum(*back_set)
    bs32[...] = total_back
    bs16[...] = total_back.astype(BF16)
    bz = pltpu.make_async_remote_copy(
        src_ref=bs16.at[1 - at.zh], dst_ref=bz_in, send_sem=bz_sem.at[0], recv_sem=bz_sem.at[1],
        device_id=partner, device_id_type=MESH,
    )
    bz.start()

    vp.finish()
    values(1)

    attended = o_scr[0, :, 0:HD] * scale[0] + o_scr[1, :, 0:HD] * scale[1]
    for h in range(HQ):
        attn_ref[:, h * HD : (h + 1) * HD] = attended[h * RL : (h + 1) * RL].astype(BF16)
    delta = jnp.sum(up32 * attended, axis=1, keepdims=True)

    ds_own = (e_own * (dot_nt(un[0], own_val) - delta * scale[0])).astype(BF16)
    dq_scr[...] = dot_nn(ds_own, rk)
    for c in range(8):
        half = c // 4
        if c % 4 == 0:
            m_scr[...] = jnp.broadcast_to(delta * scale[half], (rows, HD))
        e16 = e_scr[c]
        dp = dot_nt(un[half], v_scr[c, :, 0:HD])
        db = m_scr[...]
        ds = jnp.concatenate(
            [
                (
                    e16[:, j * HD : (j + 1) * HD].astype(F32)
                    * (dp[:, j * HD : (j + 1) * HD] - db)
                ).astype(BF16)
                for j in range(cols // HD)
            ],
            axis=1,
        )
        dq_scr[...] += dot_nn(ds, keys(c))

    dq = (dq_scr[...] * (HD ** (-0.5))).astype(BF16)
    dq_wide = jnp.concatenate([dq[h * RL : (h + 1) * RL] for h in range(HQ)], axis=1)
    qb = dot_nt(q_up, dq_wide).astype(BF16)
    down = 2.0 * dot_nn(qb, rh[...])
    q_term_up = 2.0 * dot_nn(low_q, dq_wide)
    for t in range(qtiles):
        if t < dtiles:
            tile = down[:, t * HD : (t + 1) * HD]
        else:
            tile = q_term_up[:, (t - dtiles) * HD : (t - dtiles + 1) * HD]
        for s in range(2):
            g_send[0, t // per, s, t % per] = (tile * pick[s]).astype(BF16)
    plane_start(*grad_set[0])

    vup_term = 2.0 * (
        dot_tn(o_scr[0, :, HD : HD + R].astype(BF16), un[0])
        + dot_tn(o_scr[1, :, HD : HD + R].astype(BF16), un[1])
        + dot_nn(low_v, dov)
    )
    for s in range(2):
        g_send[1, dtiles // per, s, dtiles % per] = (vup_term * pick[s]).astype(BF16)
    bz.wait_recv()
    back = (bs32[at.zh] + bz_in[...].astype(F32)).astype(BF16)
    for s in range(2):
        term = 2.0 * dot_nn(back[s][:, 0:PB], ph[s]) + vterm[...] * pick[s]
        for t in range(dtiles):
            g_send[1, t // per, s, t % per] = term[:, t * HD : (t + 1) * HD].astype(BF16)
    plane_start(*grad_set[1])

    def line_copy(i, k, sender):
        device, _ = at.line(k)
        spot = zbuf.at[i, sender]
        return pltpu.make_async_remote_copy(
            src_ref=spot, dst_ref=spot, send_sem=zl_ssem.at[i, k], recv_sem=zl_rsem.at[i, k],
            device_id=device, device_id_type=MESH,
        )

    def line_start(i):
        total = plane_sum(*grad_set[i]).astype(BF16)
        zbuf[i, at.z] = total.reshape(2 * per, R, HD)

        def body(k, _):
            line_copy(i, k, at.z).start()
            return 0

        lax.fori_loop(1, NZ, body, 0)

    def core_copy(i):
        return pltpu.make_async_remote_copy(
            src_ref=acc16.at[i, 1 - at.c], dst_ref=core_in.at[i], send_sem=c_sem.at[i, 0],
            recv_sem=c_sem.at[i, 1], device_id=at.other_core(), device_id_type=MESH,
        )

    def line_sum(i):
        def waits(k, _):
            line_copy(i, k, lax.rem(at.z + NZ - k, NZ)).wait_recv()
            return 0

        lax.fori_loop(1, NZ, waits, 0)
        acc32[i] = jnp.zeros(acc32.shape[1:], F32)

        def body(z, _):
            tag = tags[z].astype(F32)
            for s in range(2):
                data = zbuf[i, z, s * per : (s + 1) * per].astype(F32)
                for t in range(T):
                    part = data * tag[s * T + t : s * T + t + 1][None]
                    acc32[i, t // half_t, t % half_t] += part
            return 0

        lax.fori_loop(0, NZ, body, 0)
        acc16[i] = acc32[i].astype(BF16)
        core_copy(i).start()

    forwards = []

    def make_forward(i, h):
        def forward(ref, step):
            c = pltpu.make_async_remote_copy(
                src_ref=ref, dst_ref=ref, send_sem=f_sem.at[i, h, step, 0],
                recv_sem=f_sem.at[i, h, step, 1], device_id=at.other_core(), device_id_type=MESH,
            )
            c.start()
            forwards.append(c)

        return forward

    streams = [
        [
            Spread(
                at, gath.at[i, at.c, h], h, sp_send, sp_recv, (i * 2 + h) * SPREAD_SEMS,
                make_forward(i, h),
            )
            for h in range(2)
        ]
        for i in range(2)
    ]

    def gather_start(i):
        core_copy(i).wait_recv()
        final = (acc32[i, at.c] + core_in[i].astype(F32)).astype(BF16)
        for h in range(2):
            a, b = (at.x, at.y) if h == 0 else (at.y, at.x)
            gath[i, at.c, h, a, b] = final[2 * h : 2 * h + 2]
            streams[i][h].first()

    def gather_second(i):
        for h in range(2):
            streams[i][h].second()

    def gather_relay(i):
        for h in range(2):
            streams[i][h].relay()

    def gather_finish(i):
        for h in range(2):
            streams[i][h].finish()

    def out_copy(i):
        return pltpu.make_async_copy(gath.at[i], gath_hbm.at[i], out_sem.at[i])

    def gather_out(i):
        for h in range(2):
            g = streams[i][h]
            for step, d in enumerate((0, 3, 1, 2)):
                row = gath.at[i, 1 - at.c, h, lax.rem(g.a + d, 4)]
                pltpu.make_async_remote_copy(
                    src_ref=row, dst_ref=row, send_sem=f_sem.at[i, h, step, 0],
                    recv_sem=f_sem.at[i, h, step, 1], device_id=at.other_core(),
                    device_id_type=MESH,
                ).wait_recv()
        out_copy(i).start()

    lax.fori_loop(1, NZ, tag_wait, 0)
    line_start(0)
    line_start(1)
    line_sum(0)
    line_sum(1)
    gather_start(0)
    gather_start(1)
    gather_second(0)
    gather_second(1)
    gather_relay(0)
    gather_relay(1)
    gather_finish(0)
    gather_finish(1)
    gather_out(0)
    gather_out(1)

    for c in [zk, zv, bz] + pick_copies + [c for step in stat_copies for c in step] + forwards:
        c.wait_send()
    for g in [ko, kp, vo, vp] + streams[0] + streams[1]:
        g.drain()
    plane_drain(*back_set)
    for i in range(2):
        plane_drain(*grad_set[i])

        def body(k, _):
            line_copy(i, k, at.z).wait_send()
            return 0

        lax.fori_loop(1, NZ, body, 0)
        core_copy(i).wait_send()
    for i in range(2):
        out_copy(i).wait()


def widen_kernel(
    dims, gath_hbm, attn_hbm, attn_out, qd_out, qu_out, vd_out, vu_out,
    gath, qd, qu, vd, vu, in_sem, out_sem, attn_sem,
):
    (D, HD, HQ, R, T, PB, RL) = dims
    qtiles = (D + HQ * HD) // HD
    dtiles = D // HD
    per = qtiles // SIDE
    attn = pltpu.make_async_copy(attn_hbm, attn_out, attn_sem)
    parts = [(i, c, h) for c in range(2) for h in range(2) for i in range(2)]
    loads = [
        pltpu.make_async_copy(gath_hbm.at[i, c, h], gath.at[i, c, h], in_sem.at[k])
        for k, (i, c, h) in enumerate(parts)
    ]
    for load in loads:
        load.start()
    attn.start()
    stores = []
    for k, (i, c, h) in enumerate(parts):
        loads[k].wait()
        down, up = (qd, qu) if i == 0 else (vd, vu)
        down_out, up_out = (qd_out, qu_out) if i == 0 else (vd_out, vu_out)
        first = c * 4 + h * 2
        for t in range(qtiles):
            if i == 1 and t > dtiles:
                continue
            p, j = t // per, t % per
            a, b = (p // 4, p % 4) if h == 0 else (p % 4, p // 4)
            tile = gath[i, c, h, a, b, :, j].astype(F32)
            if t < dtiles:
                down[first : first + 2, :, t * HD : (t + 1) * HD] = tile
            else:
                up[first : first + 2, :, (t - dtiles) * HD : (t - dtiles + 1) * HD] = tile
        pair = pl.ds(first, 2)
        for n, (src, dst) in enumerate(((down, down_out), (up, up_out))):
            store = pltpu.make_async_copy(src.at[pair], dst.at[pair], out_sem.at[2 * k + n])
            store.start()
            stores.append(store)
    for store in stores:
        store.wait()
    attn.wait()


def per_device(
    prompt_hidden, prompt_keys, prompt_values, resp_hidden, resp_queries, resp_keys, resp_values,
    cotangent, rewards, resp_prompt, resp_len, prompt_tenant, q_down, q_up, v_down, v_up,
):
    D = prompt_hidden.shape[2]
    PB = prompt_hidden.shape[1]
    HD = prompt_keys.shape[2]
    HQ = resp_queries.shape[2] // HD
    T, _, R = q_down.shape
    RL = resp_hidden.shape[1]
    dims = (D, HD, HQ, R, T, PB, RL)
    rows = RL * HQ
    per = (D + HQ * HD) // HD // SIDE
    cols = 4 * PB
    vmem = pl.BlockSpec(memory_space=pltpu.VMEM)
    smem = pl.BlockSpec(memory_space=pltpu.SMEM)
    hbm = pl.BlockSpec(memory_space=pl.ANY)
    dma = pltpu.SemaphoreType.DMA
    gath_shape = (2, 2, 2, 4, 4, 2, per, R, HD)
    attn, gath = pl.pallas_call(
        functools.partial(step_kernel, dims),
        name="step",
        out_shape=(
            jax.ShapeDtypeStruct((RL, HQ * HD), BF16),
            jax.ShapeDtypeStruct(gath_shape, BF16),
        ),
        in_specs=[hbm] * 8 + [smem] * 4 + [hbm] * 4,
        out_specs=(vmem, hbm),
        scratch_shapes=[
            pltpu.VMEM(gath_shape, BF16),
            pltpu.VMEM((2, PB, D), BF16),
            pltpu.VMEM((RL, D), BF16),
            pltpu.VMEM((T, R, D), BF16),
            pltpu.VMEM((T, R, D), BF16),
            pltpu.VMEM((RL, HQ * HD), BF16),
            pltpu.VMEM((RL, HD), BF16),
            pltpu.VMEM((RL, HD), BF16),
            pltpu.VMEM((RL, HQ * HD), BF16),
            pltpu.VMEM((T, R, HQ * HD), BF16),
            pltpu.VMEM((T, R, HD), BF16),
            pltpu.VMEM((2, 2, 2, 2, PB, HD), BF16),
            pltpu.VMEM((2, 2, 2, 2, PB + R, HD), BF16),
            pltpu.VMEM((2, 2, 3, 2, PB, HD), BF16),
            pltpu.VMEM((2, 2, 3, 2, PB + R, HD), BF16),
            pltpu.VMEM((2, 2, 2, 2, 2, PB, HD), BF16),
            pltpu.VMEM((2, 2, 2, 2, 2, PB + R, HD), BF16),
            pltpu.VMEM((8, rows, cols), F32),
            pltpu.VMEM((8, rows, cols), BF16),
            pltpu.VMEM((8, cols, 2 * HD), BF16),
            pltpu.VMEM((rows, HD), F32),
            pltpu.VMEM((rows, HD), F32),
            pltpu.VMEM((2, rows, 2 * HD), F32),
            pltpu.VMEM((rows, HD), F32),
            pltpu.VMEM((4, 8, HD), F32),
            pltpu.VMEM((10, 8, HD), F32),
            pltpu.VMEM((SIDE, 2, 2, R, HD), BF16),
            pltpu.VMEM((SIDE, 2, 2, R, HD), BF16),
            pltpu.VMEM((2, 2, R, HD), F32),
            pltpu.VMEM((2, 2, R, HD), BF16),
            pltpu.VMEM((2, R, HD), BF16),
            pltpu.VMEM((2, SIDE, 2, per, R, HD), BF16),
            pltpu.VMEM((2, SIDE, 2, per, R, HD), BF16),
            pltpu.VMEM((2, NZ, 2 * per, R, HD), BF16),
            pltpu.VMEM((NZ, R, HD), BF16),
            pltpu.VMEM((2, 2, T // 2, per, R, HD), F32),
            pltpu.VMEM((2, 2, T // 2, per, R, HD), BF16),
            pltpu.VMEM((2, T // 2, per, R, HD), BF16),
            pltpu.VMEM((R, D), F32),
            dma((12,)),
            dma((4 * HOLD_SEMS,)),
            dma((4 * HOLD_SEMS,)),
            dma((4 * SPREAD_SEMS,)),
            dma((4 * SPREAD_SEMS,)),
            dma((2,)),
            dma((2,)),
            dma((10,)),
            dma((10,)),
            dma((SIDE,)),
            dma((SIDE,)),
            dma((2,)),
            dma((2, SIDE)),
            dma((2, SIDE)),
            dma((2, NZ)),
            dma((2, NZ)),
            dma((NZ,)),
            dma((NZ,)),
            dma((2, 2)),
            dma((2, 2, 4, 2)),
            dma((2,)),
        ],
        compiler_params=pltpu.CompilerParams(
            collective_id=0, has_side_effects=True, vmem_limit_bytes=60 * 2**20
        ),
    )(
        prompt_hidden, prompt_keys, prompt_values, resp_hidden[0], resp_queries[0], resp_keys[0],
        resp_values[0], cotangent[0], rewards, resp_prompt, resp_len, prompt_tenant,
        jnp.swapaxes(q_down, 1, 2), q_up, jnp.swapaxes(v_down, 1, 2), v_up,
    )

    shapes = ((T, R, D), (T, R, HQ * HD), (T, R, D), (T, R, HD))
    attn, qd_t, g_qu, vd_t, g_vu = pl.pallas_call(
        functools.partial(widen_kernel, dims),
        name="widen",
        out_shape=(jax.ShapeDtypeStruct((RL, HQ * HD), BF16),)
        + tuple(jax.ShapeDtypeStruct(x, F32) for x in shapes),
        in_specs=[hbm, hbm],
        out_specs=(hbm,) * 5,
        scratch_shapes=[pltpu.VMEM(gath_shape, BF16)]
        + [pltpu.VMEM(x, F32) for x in shapes]
        + [dma((8,)), dma((16,)), dma],
        compiler_params=pltpu.CompilerParams(vmem_limit_bytes=60 * 2**20),
    )(gath, attn)
    return (
        attn[None],
        jnp.swapaxes(qd_t, 1, 2),
        g_qu,
        jnp.swapaxes(vd_t, 1, 2),
        g_vu,
    )


def solution(mesh):
    rows = P("prompt", "resp", None)
    pair = P("prompt", "resp")
    return jax.shard_map(
        per_device,
        mesh=mesh,
        in_specs=(rows,) * 8 + (pair,) * 3 + (P("prompt"),) + (P(),) * 4,
        out_specs=(rows, P(), P(), P(), P()),
        check_vma=False,
    )
```

```python
import functools

import jax
import jax.numpy as jnp
from jax import lax
from jax.experimental import pallas as pl
from jax.experimental.pallas import tpu as pltpu
from jax.sharding import PartitionSpec as P

MESH = pl.DeviceIdType.MESH
F32 = jnp.float32
BF16 = jnp.bfloat16
NX = 4
NZ = 8
SIDE = NX * NX
LOG2E = 1.4426950408889634


def dot_nn(a, b):
    return lax.dot_general(a, b, (((1,), (0,)), ((), ())), preferred_element_type=F32)


def dot_nt(a, b):
    return lax.dot_general(a, b, (((1,), (1,)), ((), ())), preferred_element_type=F32)


def dot_tn(a, b):
    return lax.dot_general(a, b, (((0,), (0,)), ((), ())), preferred_element_type=F32)


class Place:
    def __init__(self):
        r = lax.axis_index("resp")
        p = lax.axis_index("prompt")
        self.x = r // 8
        self.y = lax.rem(r // 2, 4)
        self.zh = lax.rem(r, 2)
        self.zl = p // 2
        self.c = lax.rem(p, 2)
        self.z = self.zh * 4 + self.zl
        self.p = self.x * 4 + self.y

    def plane(self, dx, dy):
        x = lax.rem(self.x + dx, 4)
        y = lax.rem(self.y + dy, 4)
        return {"resp": (x * 4 + y) * 2 + self.zh}, x * 4 + y

    def line(self, dz):
        z = lax.rem(self.z + dz, NZ)
        return {
            "prompt": lax.rem(z, 4) * 2 + self.c,
            "resp": self.p * 2 + z // 4,
        }, z

    def other_core(self):
        return {"prompt": self.zl * 2 + (1 - self.c)}

    def along(self, axis, d):
        return self.plane(d, 0)[0] if axis == 0 else self.plane(0, d)[0]


class Spread:
    def __init__(self, at, buf, axis, send, recv, base, forward=None):
        self.at = at
        self.buf = buf
        self.axis = axis
        self.a = at.x if axis == 0 else at.y
        self.b = at.y if axis == 0 else at.x
        self.send = send
        self.recv = recv
        self.base = base
        self.sent = []
        self.forward = forward or (lambda ref, step: None)

    def copy(self, src, dst, sem, device):
        return pltpu.make_async_remote_copy(
            src_ref=src,
            dst_ref=dst,
            send_sem=self.send.at[self.base + sem],
            recv_sem=self.recv.at[self.base + sem],
            device_id=device,
            device_id_type=MESH,
        )

    def push(self, ref, sem, device):
        c = self.copy(ref, ref, sem, device)
        c.start()
        self.sent.append(c)

    def take(self, ref, sem, device):
        self.copy(ref, ref, sem, device).wait_recv()

    def first(self):
        mine = self.buf.at[self.a, self.b]
        for d in (1, 3, 2):
            self.push(mine, d - 1, self.at.along(1 - self.axis, d))

    def second(self):
        for d in (1, 3, 2):
            self.take(
                self.buf.at[self.a, lax.rem(self.b + 4 - d, 4)],
                d - 1,
                self.at.along(1 - self.axis, d),
            )
        row = self.buf.at[self.a]
        self.push(row, 3, self.at.along(self.axis, 1))
        self.push(row, 4, self.at.along(self.axis, 3))
        self.forward(row, 0)

    def relay(self):
        low = lax.rem(self.a + 3, 4)
        high = lax.rem(self.a + 1, 4)
        self.take(self.buf.at[low], 3, self.at.along(self.axis, 1))
        self.push(self.buf.at[low, pl.ds(0, 2)], 5, self.at.along(self.axis, 1))
        self.forward(self.buf.at[low], 1)
        self.take(self.buf.at[high], 4, self.at.along(self.axis, 3))
        self.push(self.buf.at[high, pl.ds(2, 2)], 6, self.at.along(self.axis, 3))
        self.forward(self.buf.at[high], 2)

    def finish(self):
        far = lax.rem(self.a + 2, 4)
        self.take(self.buf.at[far, pl.ds(0, 2)], 5, self.at.along(self.axis, 1))
        self.take(self.buf.at[far, pl.ds(2, 2)], 6, self.at.along(self.axis, 3))
        self.forward(self.buf.at[far], 3)

    def drain(self):
        for c in self.sent:
            c.wait_send()


SPREAD_SEMS = 7
HOLD_SEMS = 9


class Hold:
    def __init__(self, at, raw, sel, out, send, recv, base):
        self.at = at
        self.raw = raw
        self.sel = sel
        self.out = out
        self.send = send
        self.recv = recv
        self.base = base
        self.par = lax.rem(at.x + at.y, 2)
        self.sent = []

    def copy(self, src, dst, sem, device):
        return pltpu.make_async_remote_copy(
            src_ref=src,
            dst_ref=dst,
            send_sem=self.send.at[self.base + sem],
            recv_sem=self.recv.at[self.base + sem],
            device_id=device,
            device_id_type=MESH,
        )

    def spot(self, par, x, y):
        return par, par * (x // 2) + (1 - par) * (y // 2)

    def mine(self):
        return self.raw.at[self.spot(self.par, self.at.x, self.at.y)]

    def columns(self, x):
        return self.out.at[lax.rem(x, 2), x // 2, lax.rem(x, 2)]

    def rows(self, y):
        return self.out.at[1 - lax.rem(y, 2), :, lax.rem(y, 2), y // 2]

    def first(self):
        mine = self.mine()
        for d in (1, 3, 2):
            c = self.copy(mine, mine, d - 1, self.at.plane(d * self.par, d * (1 - self.par))[0])
            c.start()
            self.sent.append(c)

    def second(self, picks, own):
        at = self.at
        for d in (1, 3, 2):
            par = lax.rem(self.par + d, 2)
            x = lax.rem(at.x + (4 - d) * par, 4)
            y = lax.rem(at.y + (4 - d) * (1 - par), 4)
            spot = self.raw.at[self.spot(par, x, y)]
            self.copy(spot, spot, d - 1, at.along(0, d)).wait_recv()
        for d in (1, 3, 2):
            for axis in range(2):
                p = picks(axis, d)
                self.sel[axis, d - 1] = self.raw[axis, :, 0] * p[0] + self.raw[axis, :, 1] * p[1]
                target = self.columns(at.x) if axis == 0 else self.rows(at.y)
                c = self.copy(self.sel.at[axis, d - 1], target, 3 + axis * 3 + d - 1, at.along(axis, d))
                c.start()
                self.sent.append(c)
        chosen = [self.raw[axis, :, 0] * own[0] + self.raw[axis, :, 1] * own[1] for axis in range(2)]
        self.out[lax.rem(at.x, 2), at.x // 2, lax.rem(at.x, 2)] = chosen[0]
        for i in range(2):
            self.out[1 - lax.rem(at.y, 2), i, lax.rem(at.y, 2), at.y // 2] = chosen[1][i]

    def finish(self):
        at = self.at
        for d in (1, 3, 2):
            spot = self.columns(lax.rem(at.x + 4 - d, 4))
            self.copy(spot, spot, 3 + d - 1, at.along(0, d)).wait_recv()
            spot = self.rows(lax.rem(at.y + 4 - d, 4))
            self.copy(spot, spot, 6 + d - 1, at.along(1, d)).wait_recv()

    def drain(self):
        for c in self.sent:
            c.wait_send()


def step_kernel(
    dims,
    ph_hbm, pk_hbm, pv_hbm, rh_hbm, rq_hbm, rk_hbm, rv_hbm, cot_hbm,
    rew_ref, rp_ref, rl_ref, pt_ref, qd_hbm, qu_hbm, vd_hbm, vu_hbm,
    attn_ref, gath,
    ph, rh, qd, vd, rq_ref, rk_ref, rv_ref, cot_ref, qu_ref, vu_ref,
    k_raw, v_raw, k_sel, v_sel, k_all, v_all,
    s_scr, e_scr, v_scr, m_scr, l_scr, o_scr, dq_scr,
    stat, stat_in,
    rsb, rsr, bs32, bs16, bz_in,
    g_send, g_in, zbuf, tags, acc32, acc16, core_in, vterm,
    load_sem, h_send, h_recv, sp_send, sp_recv, z_send, z_recv, st_send, st_recv,
    rs_send, rs_recv, bz_sem, g_ssem, g_rsem, zl_ssem, zl_rsem, tag_ssem, tag_rsem, c_sem, f_sem,
):
    (D, HD, HQ, R, T, PB, RL) = dims
    at = Place()
    rows = RL * HQ
    qtiles = (D + HQ * HD) // HD
    dtiles = D // HD
    per = qtiles // SIDE
    half_t = T // 2

    barrier = pltpu.get_barrier_semaphore()

    def greet_plane(k, _):
        pl.semaphore_signal(
            barrier, inc=1, device_id=at.plane(k // 4, lax.rem(k, 4))[0], device_id_type=MESH
        )
        return 0

    def greet_line(k, _):
        pl.semaphore_signal(barrier, inc=1, device_id=at.line(k)[0], device_id_type=MESH)
        return 0

    lax.fori_loop(1, SIDE, greet_plane, 0)
    lax.fori_loop(1, NZ, greet_line, 0)
    pl.semaphore_signal(barrier, inc=1, device_id=at.other_core(), device_id_type=MESH)

    par = lax.rem(at.x + at.y, 2)
    place = par * (at.x // 2) + (1 - par) * (at.y // 2)
    loads = [
        pltpu.make_async_copy(s, d, load_sem.at[i])
        for i, (s, d) in enumerate(
            (
                (pk_hbm, k_raw.at[0, par, place]),
                (pv_hbm, v_raw.at[0, par, place, :, pl.ds(0, PB)]),
                (ph_hbm, ph),
                (vd_hbm, vd),
                (rh_hbm, rh),
                (qd_hbm, qd),
                (rq_hbm, rq_ref),
                (qu_hbm, qu_ref),
                (vu_hbm, vu_ref),
                (rk_hbm, rk_ref),
                (rv_hbm, rv_ref),
                (cot_hbm, cot_ref),
            )
        )
    ]
    for c in loads:
        c.start()

    for s in range(2):
        v_raw[0, par, place, s, PB : PB + R, :] = jnp.zeros((R, HD), BF16)
    rsb[...] = jnp.zeros(rsb.shape, BF16)
    for t in range(dtiles + 1, qtiles):
        for s in range(2):
            g_send[1, t // per, s, t % per] = jnp.zeros((R, HD), BF16)

    chosen = rp_ref[0, 0]
    length = rl_ref[0, 0]
    reward = rew_ref[0, 0]
    pick = [(chosen == s).astype(F32) for s in range(2)]
    ten = [pt_ref[0], pt_ref[1]]
    own_ten = jnp.where(chosen == 0, ten[0], ten[1])

    row8 = lax.broadcasted_iota(jnp.int32, (8, HD), 0)
    stat[0] = jnp.where(
        row8 == 0,
        reward * pick[0],
        jnp.where(
            row8 == 1,
            reward * pick[1],
            jnp.where(row8 == 2, pick[0], jnp.where(row8 == 3, pick[1], 0.0)),
        ),
    )

    loads[0].wait()
    pl.semaphore_wait(barrier, SIDE - 1 + NZ - 1 + 1)

    def hold(raw, sel, out, z, i):
        return Hold(at, raw.at[z], sel.at[z], out.at[z], h_send, h_recv, i * HOLD_SEMS)

    ko, kp = [hold(k_raw, k_sel, k_all, z, z) for z in range(2)]
    vo, vp = [hold(v_raw, v_sel, v_all, z, 2 + z) for z in range(2)]
    partner = at.line(4)[0]

    def across(raw, i):
        return pltpu.make_async_remote_copy(
            src_ref=raw.at[0, par, place], dst_ref=raw.at[1, par, place],
            send_sem=z_send.at[i], recv_sem=z_recv.at[i],
            device_id=partner, device_id_type=MESH,
        )

    zk = across(k_raw, 0)
    zv = across(v_raw, 1)
    zk.start()
    ko.first()

    def stat_copy(step, d):
        i = step * 3 + d - 1
        device = partner if step == 2 else at.along(step, d)
        return pltpu.make_async_remote_copy(
            src_ref=stat.at[step], dst_ref=stat_in.at[i],
            send_sem=st_send.at[i], recv_sem=st_recv.at[i],
            device_id=device, device_id_type=MESH,
        )

    def pick_copy(d):
        return pltpu.make_async_remote_copy(
            src_ref=stat.at[0], dst_ref=stat_in.at[6 + d],
            send_sem=st_send.at[6 + d], recv_sem=st_recv.at[6 + d],
            device_id=at.along(1, d), device_id_type=MESH,
        )

    stat_copies = [[stat_copy(0, d) for d in (1, 2, 3)], [stat_copy(1, d) for d in (1, 2, 3)], [stat_copy(2, 1)]]
    pick_copies = [pick_copy(d) for d in (1, 2, 3)]

    def stat_start(step):
        for c in stat_copies[step]:
            c.start()

    def stat_sum(step):
        total = stat[step]
        for i, c in enumerate(stat_copies[step]):
            c.wait_recv()
            total = total + stat_in[step * 3 + i]
        stat[step + 1] = total

    def picks(axis, d):
        tile = stat_in[(0 if axis == 0 else 7) + 3 - d].astype(BF16)
        return [tile[2 + s : 3 + s] for s in range(2)]

    own_pick = [stat[0].astype(BF16)[2 + s : 3 + s] for s in range(2)]

    stat_start(0)
    for c in pick_copies:
        c.start()
    for i in (1, 2, 3):
        loads[i].wait()
    for s in range(2):
        low = dot_nt(vd[ten[s]], ph[s]).astype(BF16)
        v_raw[0, par, place, s, PB : PB + R, 0:PB] = low

    vo.first()
    zv.start()

    r16 = lax.broadcasted_iota(jnp.int32, (R, HD), 0)
    owner = jnp.where(r16 < T, ten[0], ten[1])
    mask = (owner == lax.rem(r16, T)).astype(F32).astype(BF16)

    tags[at.z] = mask

    def tag_copy(k, sender):
        spot = tags.at[sender]
        return pltpu.make_async_remote_copy(
            src_ref=spot, dst_ref=spot, send_sem=tag_ssem.at[k], recv_sem=tag_rsem.at[k],
            device_id=at.line(k)[0], device_id_type=MESH,
        )

    def tag_start(k, _):
        tag_copy(k, at.z).start()
        return 0

    def tag_wait(k, _):
        tag_copy(k, at.z).wait_send()
        tag_copy(k, lax.rem(at.z + NZ - k, NZ)).wait_recv()
        return 0

    for c in loads[4:]:
        c.wait()
    low_qv = dot_nt(jnp.concatenate([qd[own_ten], vd[own_ten]], axis=0), rh[...]).astype(BF16)
    low_q = low_qv[0:R]
    low_v = low_qv[R : 2 * R]
    q_up = qu_ref[own_ten]
    v_up = vu_ref[own_ten]
    queries = (rq_ref[...].astype(F32) + 2.0 * dot_tn(low_q, q_up)).astype(BF16)
    own_val = (rv_ref[...].astype(F32) + 2.0 * dot_tn(low_v, v_up)).astype(BF16)
    qh = jnp.concatenate([queries[:, h * HD : (h + 1) * HD] for h in range(HQ)], axis=0)
    rk = rk_ref[...]
    stat_sum(0)
    for c in pick_copies:
        c.wait_recv()
    ko.second(picks, own_pick)
    stat_start(1)
    vo.second(picks, own_pick)

    factor = HD ** (-0.5) * LOG2E
    s_own = dot_nt(qh, rk)
    q_pos = lax.rem(lax.broadcasted_iota(jnp.int32, (rows, RL), 0), RL)
    k_pos = lax.broadcasted_iota(jnp.int32, (rows, RL), 1)
    allowed = (k_pos <= q_pos) & (k_pos < length)
    m_own = jnp.max(jnp.where(allowed, s_own, -1e30), axis=1, keepdims=True)

    zk.wait_recv()
    kp.first()
    lax.fori_loop(1, NZ, tag_start, 0)
    stat_sum(1)
    stat_start(2)
    ko.finish()

    cols = 4 * PB
    row_r = lax.broadcasted_iota(jnp.int32, (R, HD), 0)
    col_r = lax.broadcasted_iota(jnp.int32, (R, HD), 1)
    lift = jnp.concatenate(
        [2.0 * v_up.astype(F32), (row_r == col_r).astype(F32)], axis=1
    ).astype(BF16)

    def keys(c):
        return k_all[c // 4, (c % 4) // 2, c % 2].reshape(cols, HD)

    def low_rows(c):
        return jnp.concatenate(
            [v_all[c // 4, (c % 4) // 2, c % 2, j // 2, j % 2, PB : PB + R, :] for j in range(4)], axis=1
        )

    def scores(half, start):
        m_scr[...] = jnp.broadcast_to(start, (rows, HD))
        for c in range(4 * half, 4 * half + 4):
            sc = dot_nt(qh, keys(c))
            s_scr[c] = sc
            top = sc[:, 0:HD]
            for j in range(1, cols // HD):
                top = jnp.maximum(top, sc[:, j * HD : (j + 1) * HD])
            m_scr[...] = jnp.maximum(m_scr[...], top)
        top = jnp.max(m_scr[...], axis=1, keepdims=True) * factor
        m_scr[...] = jnp.broadcast_to(top, (rows, HD))
        return top

    def exps(half):
        l_scr[...] = jnp.zeros((rows, HD), F32)
        for c in range(4 * half, 4 * half + 4):
            sc = s_scr[c]
            mb = m_scr[...]
            part = l_scr[...]
            for j in range(cols // HD):
                ex = jnp.exp2(sc[:, j * HD : (j + 1) * HD] * factor - mb)
                part = part + ex
                e_scr[c, :, j * HD : (j + 1) * HD] = ex.astype(BF16)
            l_scr[...] = part
        return jnp.sum(l_scr[...], axis=1, keepdims=True)

    def values(half):
        for c in range(4 * half, 4 * half + 4):
            ext = dot_tn(low_rows(c), lift)
            blk = v_all[c // 4, (c % 4) // 2, c % 2, :, :, 0:PB, :].reshape(4, PB, HD)
            for j in range(4):
                v_scr[c, j * PB : (j + 1) * PB, 0:HD] = (
                    blk[j].astype(F32) + ext[j * HD : j * HD + PB, 0:HD]
                ).astype(BF16)
                v_scr[c, j * PB : (j + 1) * PB, HD : 2 * HD] = ext[
                    j * HD : j * HD + PB, HD : 2 * HD
                ].astype(BF16)
            o_scr[half] += dot_nn(e_scr[c], v_scr[c])

    top0 = scores(0, m_own)
    kp.second(picks, own_pick)
    l0 = exps(0)
    e_own = jnp.where(allowed, jnp.exp2(s_own * factor - top0), 0.0)
    e_own16 = e_own.astype(BF16)
    l0 = l0 + jnp.sum(e_own, axis=1, keepdims=True)
    zv.wait_recv()
    vp.first()
    o_scr[0, :, 0:HD] = dot_nn(e_own16, own_val)
    o_scr[0, :, HD : 2 * HD] = jnp.zeros((rows, HD), F32)
    o_scr[1] = jnp.zeros((rows, 2 * HD), F32)
    vo.finish()
    values(0)

    stat_sum(2)
    st = stat[3]
    mean = pick[0] * st[0:1] / jnp.maximum(st[2:3], 1.0) + pick[1] * st[1:2] / jnp.maximum(st[3:4], 1.0)
    weight = -(reward - mean) / RL
    live = (lax.broadcasted_iota(jnp.int32, (RL, HD), 0) < length).astype(F32) * weight
    ct = cot_ref[...].astype(F32)
    up = jnp.concatenate(
        [(ct[:, h * HD : (h + 1) * HD] * live).astype(BF16) for h in range(HQ)], axis=0
    )
    up32 = up.astype(F32)

    kp.finish()
    top1 = scores(1, jnp.full((rows, 1), -1e30, F32))
    vp.second(picks, own_pick)
    l1 = exps(1)
    top = jnp.maximum(top0, top1)
    share0 = jnp.exp2(top0 - top)
    share1 = jnp.exp2(top1 - top)
    inv = 1.0 / (share0 * l0 + share1 * l1)
    scale = [share0 * inv, share1 * inv]
    un = [(up32 * scale[h]).astype(BF16) for h in range(2)]

    for c in range(8):
        half = c // 4
        if c % 4 == 0:
            uv = dot_nt(v_up, un[half]).astype(BF16)
        x = (c % 2) * 2 + (c % 4) // 2
        back = dot_nn(uv, e_scr[c])
        z = at.zh if half == 0 else 1 - at.zh
        for j in range(4):
            y = (j % 2) * 2 + j // 2
            piece = back[:, j * PB : (j + 1) * PB]
            for s in range(2):
                rsb[x * 4 + y, z, s, :, 0:PB] = (piece * pick[s]).astype(BF16)

    def plane_copy(src, dst, send, recv, k):
        device, p = at.plane(k // 4, lax.rem(k, 4))
        return pltpu.make_async_remote_copy(
            src_ref=src.at[p], dst_ref=dst.at[k], send_sem=send.at[k], recv_sem=recv.at[k],
            device_id=device, device_id_type=MESH,
        )

    def plane_start(src, dst, send, recv):
        def body(k, _):
            plane_copy(src, dst, send, recv, k).start()
            return 0

        lax.fori_loop(1, SIDE, body, 0)

    def plane_sum(src, dst, send, recv):
        def body(k, total):
            plane_copy(src, dst, send, recv, k).wait_recv()
            return total + dst[k].astype(F32)

        return lax.fori_loop(1, SIDE, body, src[at.p].astype(F32))

    def plane_drain(src, dst, send, recv):
        def body(k, _):
            plane_copy(src, dst, send, recv, k).wait_send()
            return 0

        lax.fori_loop(1, SIDE, body, 0)

    back_set = (rsb, rsr, rs_send, rs_recv)
    grad_set = [(g_send.at[i], g_in.at[i], g_ssem.at[i], g_rsem.at[i]) for i in range(2)]
    plane_start(*back_set)

    dov = dot_tn(e_own16, un[0]).astype(BF16)
    vb = dot_nt(v_up, dov).astype(BF16)
    vterm[...] = 2.0 * dot_nn(vb, rh[...])
    vp.finish()
    values(1)

    attended = o_scr[0, :, 0:HD] * scale[0] + o_scr[1, :, 0:HD] * scale[1]
    for h in range(HQ):
        attn_ref[:, h * HD : (h + 1) * HD] = attended[h * RL : (h + 1) * RL].astype(BF16)
    delta = jnp.sum(up32 * attended, axis=1, keepdims=True)

    total_back = plane_sum(*back_set)
    bs32[...] = total_back
    bs16[...] = total_back.astype(BF16)
    bz = pltpu.make_async_remote_copy(
        src_ref=bs16.at[1 - at.zh], dst_ref=bz_in, send_sem=bz_sem.at[0], recv_sem=bz_sem.at[1],
        device_id=partner, device_id_type=MESH,
    )
    bz.start()

    ds_own = (e_own * (dot_nt(un[0], own_val) - delta * scale[0])).astype(BF16)
    dq_scr[...] = dot_nn(ds_own, rk)
    for c in range(8):
        half = c // 4
        if c % 4 == 0:
            m_scr[...] = jnp.broadcast_to(delta * scale[half], (rows, HD))
        e16 = e_scr[c]
        dp = dot_nt(un[half], v_scr[c, :, 0:HD])
        db = m_scr[...]
        ds = jnp.concatenate(
            [
                (
                    e16[:, j * HD : (j + 1) * HD].astype(F32)
                    * (dp[:, j * HD : (j + 1) * HD] - db)
                ).astype(BF16)
                for j in range(cols // HD)
            ],
            axis=1,
        )
        dq_scr[...] += dot_nn(ds, keys(c))

    dq = (dq_scr[...] * (HD ** (-0.5))).astype(BF16)
    dq_wide = jnp.concatenate([dq[h * RL : (h + 1) * RL] for h in range(HQ)], axis=1)
    qb = dot_nt(q_up, dq_wide).astype(BF16)
    down = 2.0 * dot_nn(qb, rh[...])
    q_term_up = 2.0 * dot_nn(low_q, dq_wide)
    for t in range(qtiles):
        if t < dtiles:
            tile = down[:, t * HD : (t + 1) * HD]
        else:
            tile = q_term_up[:, (t - dtiles) * HD : (t - dtiles + 1) * HD]
        for s in range(2):
            g_send[0, t // per, s, t % per] = (tile * pick[s]).astype(BF16)
    plane_start(*grad_set[0])

    vup_term = 2.0 * (
        dot_tn(o_scr[0, :, HD : HD + R].astype(BF16), un[0])
        + dot_tn(o_scr[1, :, HD : HD + R].astype(BF16), un[1])
        + dot_nn(low_v, dov)
    )
    for s in range(2):
        g_send[1, dtiles // per, s, dtiles % per] = (vup_term * pick[s]).astype(BF16)
    bz.wait_recv()
    back = (bs32[at.zh] + bz_in[...].astype(F32)).astype(BF16)
    for s in range(2):
        term = 2.0 * dot_nn(back[s][:, 0:PB], ph[s]) + vterm[...] * pick[s]
        for t in range(dtiles):
            g_send[1, t // per, s, t % per] = term[:, t * HD : (t + 1) * HD].astype(BF16)
    plane_start(*grad_set[1])

    def line_copy(i, k, sender):
        device, _ = at.line(k)
        spot = zbuf.at[i, sender]
        return pltpu.make_async_remote_copy(
            src_ref=spot, dst_ref=spot, send_sem=zl_ssem.at[i, k], recv_sem=zl_rsem.at[i, k],
            device_id=device, device_id_type=MESH,
        )

    def line_start(i):
        total = plane_sum(*grad_set[i]).astype(BF16)
        zbuf[i, at.z] = total.reshape(2 * per, R, HD)

        def body(k, _):
            line_copy(i, k, at.z).start()
            return 0

        lax.fori_loop(1, NZ, body, 0)

    def core_copy(i):
        return pltpu.make_async_remote_copy(
            src_ref=acc16.at[i, 1 - at.c], dst_ref=core_in.at[i], send_sem=c_sem.at[i, 0],
            recv_sem=c_sem.at[i, 1], device_id=at.other_core(), device_id_type=MESH,
        )

    def line_sum(i):
        def waits(k, _):
            line_copy(i, k, lax.rem(at.z + NZ - k, NZ)).wait_recv()
            return 0

        lax.fori_loop(1, NZ, waits, 0)
        tag = [tags[z].astype(F32) for z in range(NZ)]
        for j in range(per):
            data = [[zbuf[i, z, n * per + j].astype(F32) for n in range(2)] for z in range(NZ)]
            for t in range(T):
                part = sum(
                    data[z][n] * tag[z][n * T + t : n * T + t + 1] for z in range(NZ) for n in range(2)
                )
                acc32[i, t // half_t, t % half_t, j] = part
                acc16[i, t // half_t, t % half_t, j] = part.astype(BF16)
        core_copy(i).start()

    forwards = []

    def make_forward(i, h):
        def forward(ref, step):
            c = pltpu.make_async_remote_copy(
                src_ref=ref, dst_ref=ref, send_sem=f_sem.at[i, h, step, 0],
                recv_sem=f_sem.at[i, h, step, 1], device_id=at.other_core(), device_id_type=MESH,
            )
            c.start()
            forwards.append(c)

        return forward

    streams = [
        [
            Spread(
                at, gath.at[i, at.c, h], h, sp_send, sp_recv, (i * 2 + h) * SPREAD_SEMS,
                make_forward(i, h),
            )
            for h in range(2)
        ]
        for i in range(2)
    ]

    def gather_start(i):
        core_copy(i).wait_recv()
        final = (acc32[i, at.c] + core_in[i].astype(F32)).astype(BF16)
        for h in range(2):
            a, b = (at.x, at.y) if h == 0 else (at.y, at.x)
            gath[i, at.c, h, a, b] = final[2 * h : 2 * h + 2]
            streams[i][h].first()

    def gather_second(i):
        for h in range(2):
            streams[i][h].second()

    def gather_relay(i):
        for h in range(2):
            streams[i][h].relay()

    def gather_finish(i):
        for h in range(2):
            streams[i][h].finish()

    def gather_out(i):
        for h in range(2):
            g = streams[i][h]
            for step, d in enumerate((0, 3, 1, 2)):
                row = gath.at[i, 1 - at.c, h, lax.rem(g.a + d, 4)]
                pltpu.make_async_remote_copy(
                    src_ref=row, dst_ref=row, send_sem=f_sem.at[i, h, step, 0],
                    recv_sem=f_sem.at[i, h, step, 1], device_id=at.other_core(),
                    device_id_type=MESH,
                ).wait_recv()

    lax.fori_loop(1, NZ, tag_wait, 0)
    line_start(0)
    line_start(1)
    line_sum(0)
    line_sum(1)
    gather_start(0)
    gather_start(1)
    gather_second(0)
    gather_second(1)
    gather_relay(0)
    gather_relay(1)
    gather_finish(0)
    gather_finish(1)
    gather_out(0)
    gather_out(1)

    for c in [zk, zv, bz] + pick_copies + [c for step in stat_copies for c in step] + forwards:
        c.wait_send()
    for g in [ko, kp, vo, vp] + streams[0] + streams[1]:
        g.drain()
    plane_drain(*back_set)
    for i in range(2):
        plane_drain(*grad_set[i])

        def body(k, _):
            line_copy(i, k, at.z).wait_send()
            return 0

        lax.fori_loop(1, NZ, body, 0)
        core_copy(i).wait_send()


def widen_kernel(
    dims, gath, attn_in, attn_out, qd_out, qu_out, vd_out, vu_out,
    qd, qu, vd, vu, out_sem, attn_sem,
):
    (D, HD, HQ, R, T, PB, RL) = dims
    qtiles = (D + HQ * HD) // HD
    dtiles = D // HD
    per = qtiles // SIDE
    attn = pltpu.make_async_copy(attn_in, attn_out, attn_sem)
    parts = [(i, c, h) for c in range(2) for h in range(2) for i in range(2)]
    attn.start()
    stores = []
    for k, (i, c, h) in enumerate(parts):
        down, up = (qd, qu) if i == 0 else (vd, vu)
        down_out, up_out = (qd_out, qu_out) if i == 0 else (vd_out, vu_out)
        first = c * 4 + h * 2
        for t in range(qtiles):
            if i == 1 and t > dtiles:
                continue
            p, j = t // per, t % per
            a, b = (p // 4, p % 4) if h == 0 else (p % 4, p // 4)
            tile = gath[i, c, h, a, b, :, j].astype(F32)
            if t < dtiles:
                down[first : first + 2, :, t * HD : (t + 1) * HD] = tile
            else:
                up[first : first + 2, :, (t - dtiles) * HD : (t - dtiles + 1) * HD] = tile
        pair = pl.ds(first, 2)
        for n, (src, dst) in enumerate(((down, down_out), (up, up_out))):
            store = pltpu.make_async_copy(src.at[pair], dst.at[pair], out_sem.at[2 * k + n])
            store.start()
            stores.append(store)
    for store in stores:
        store.wait()
    attn.wait()


def per_device(
    prompt_hidden, prompt_keys, prompt_values, resp_hidden, resp_queries, resp_keys, resp_values,
    cotangent, rewards, resp_prompt, resp_len, prompt_tenant, q_down, q_up, v_down, v_up,
):
    D = prompt_hidden.shape[2]
    PB = prompt_hidden.shape[1]
    HD = prompt_keys.shape[2]
    HQ = resp_queries.shape[2] // HD
    T, _, R = q_down.shape
    RL = resp_hidden.shape[1]
    dims = (D, HD, HQ, R, T, PB, RL)
    rows = RL * HQ
    per = (D + HQ * HD) // HD // SIDE
    cols = 4 * PB
    vmem = pl.BlockSpec(memory_space=pltpu.VMEM)
    smem = pl.BlockSpec(memory_space=pltpu.SMEM)
    hbm = pl.BlockSpec(memory_space=pl.ANY)
    dma = pltpu.SemaphoreType.DMA
    gath_shape = (2, 2, 2, 4, 4, 2, per, R, HD)
    attn, gath = pl.pallas_call(
        functools.partial(step_kernel, dims),
        name="step",
        out_shape=(
            pltpu.VMEM((RL, HQ * HD), BF16),
            pltpu.VMEM(gath_shape, BF16),
        ),
        in_specs=[hbm] * 8 + [smem] * 4 + [hbm] * 4,
        out_specs=(vmem, vmem),
        scratch_shapes=[
            pltpu.VMEM((2, PB, D), BF16),
            pltpu.VMEM((RL, D), BF16),
            pltpu.VMEM((T, R, D), BF16),
            pltpu.VMEM((T, R, D), BF16),
            pltpu.VMEM((RL, HQ * HD), BF16),
            pltpu.VMEM((RL, HD), BF16),
            pltpu.VMEM((RL, HD), BF16),
            pltpu.VMEM((RL, HQ * HD), BF16),
            pltpu.VMEM((T, R, HQ * HD), BF16),
            pltpu.VMEM((T, R, HD), BF16),
            pltpu.VMEM((2, 2, 2, 2, PB, HD), BF16),
            pltpu.VMEM((2, 2, 2, 2, PB + R, HD), BF16),
            pltpu.VMEM((2, 2, 3, 2, PB, HD), BF16),
            pltpu.VMEM((2, 2, 3, 2, PB + R, HD), BF16),
            pltpu.VMEM((2, 2, 2, 2, 2, PB, HD), BF16),
            pltpu.VMEM((2, 2, 2, 2, 2, PB + R, HD), BF16),
            pltpu.VMEM((8, rows, cols), F32),
            pltpu.VMEM((8, rows, cols), BF16),
            pltpu.VMEM((8, cols, 2 * HD), BF16),
            pltpu.VMEM((rows, HD), F32),
            pltpu.VMEM((rows, HD), F32),
            pltpu.VMEM((2, rows, 2 * HD), F32),
            pltpu.VMEM((rows, HD), F32),
            pltpu.VMEM((4, 8, HD), F32),
            pltpu.VMEM((10, 8, HD), F32),
            pltpu.VMEM((SIDE, 2, 2, R, HD), BF16),
            pltpu.VMEM((SIDE, 2, 2, R, HD), BF16),
            pltpu.VMEM((2, 2, R, HD), F32),
            pltpu.VMEM((2, 2, R, HD), BF16),
            pltpu.VMEM((2, R, HD), BF16),
            pltpu.VMEM((2, SIDE, 2, per, R, HD), BF16),
            pltpu.VMEM((2, SIDE, 2, per, R, HD), BF16),
            pltpu.VMEM((2, NZ, 2 * per, R, HD), BF16),
            pltpu.VMEM((NZ, R, HD), BF16),
            pltpu.VMEM((2, 2, T // 2, per, R, HD), F32),
            pltpu.VMEM((2, 2, T // 2, per, R, HD), BF16),
            pltpu.VMEM((2, T // 2, per, R, HD), BF16),
            pltpu.VMEM((R, D), F32),
            dma((12,)),
            dma((4 * HOLD_SEMS,)),
            dma((4 * HOLD_SEMS,)),
            dma((4 * SPREAD_SEMS,)),
            dma((4 * SPREAD_SEMS,)),
            dma((2,)),
            dma((2,)),
            dma((10,)),
            dma((10,)),
            dma((SIDE,)),
            dma((SIDE,)),
            dma((2,)),
            dma((2, SIDE)),
            dma((2, SIDE)),
            dma((2, NZ)),
            dma((2, NZ)),
            dma((NZ,)),
            dma((NZ,)),
            dma((2, 2)),
            dma((2, 2, 4, 2)),
        ],
        compiler_params=pltpu.CompilerParams(
            collective_id=0, has_side_effects=True, vmem_limit_bytes=58 * 2**20
        ),
    )(
        prompt_hidden, prompt_keys, prompt_values, resp_hidden[0], resp_queries[0], resp_keys[0],
        resp_values[0], cotangent[0], rewards, resp_prompt, resp_len, prompt_tenant,
        jnp.swapaxes(q_down, 1, 2), q_up, jnp.swapaxes(v_down, 1, 2), v_up,
    )

    shapes = ((T, R, D), (T, R, HQ * HD), (T, R, D), (T, R, HD))
    attn, qd_t, g_qu, vd_t, g_vu = pl.pallas_call(
        functools.partial(widen_kernel, dims),
        name="widen",
        out_shape=(jax.ShapeDtypeStruct((RL, HQ * HD), BF16),)
        + tuple(jax.ShapeDtypeStruct(x, F32) for x in shapes),
        in_specs=[vmem, vmem],
        out_specs=(hbm,) * 5,
        scratch_shapes=[pltpu.VMEM(x, F32) for x in shapes]
        + [dma((16,)), dma],
        compiler_params=pltpu.CompilerParams(vmem_limit_bytes=40 * 2**20),
    )(gath, attn)
    return (
        attn[None],
        jnp.swapaxes(qd_t, 1, 2),
        g_qu,
        jnp.swapaxes(vd_t, 1, 2),
        g_vu,
    )


def solution(mesh):
    rows = P("prompt", "resp", None)
    pair = P("prompt", "resp")
    return jax.shard_map(
        per_device,
        mesh=mesh,
        in_specs=(rows,) * 8 + (pair,) * 3 + (P("prompt"),) + (P(),) * 4,
        out_specs=(rows, P(), P(), P(), P()),
        check_vma=False,
    )
```

```python
import functools

import jax
import jax.numpy as jnp
from jax import lax
from jax.experimental import pallas as pl
from jax.experimental.pallas import tpu as pltpu
from jax.sharding import PartitionSpec as P

MESH = pl.DeviceIdType.MESH
F32 = jnp.float32
BF16 = jnp.bfloat16
NX = 4
NZ = 8
SIDE = NX * NX
LOG2E = 1.4426950408889634


def dot_nn(a, b):
    return lax.dot_general(a, b, (((1,), (0,)), ((), ())), preferred_element_type=F32)


def dot_nt(a, b):
    return lax.dot_general(a, b, (((1,), (1,)), ((), ())), preferred_element_type=F32)


def dot_tn(a, b):
    return lax.dot_general(a, b, (((0,), (0,)), ((), ())), preferred_element_type=F32)


class Place:
    def __init__(self):
        r = lax.axis_index("resp")
        p = lax.axis_index("prompt")
        self.x = r // 8
        self.y = lax.rem(r // 2, 4)
        self.zh = lax.rem(r, 2)
        self.zl = p // 2
        self.c = lax.rem(p, 2)
        self.z = self.zh * 4 + self.zl
        self.p = self.x * 4 + self.y

    def plane(self, dx, dy):
        x = lax.rem(self.x + dx, 4)
        y = lax.rem(self.y + dy, 4)
        return {"resp": (x * 4 + y) * 2 + self.zh}, x * 4 + y

    def line(self, dz):
        z = lax.rem(self.z + dz, NZ)
        return {
            "prompt": lax.rem(z, 4) * 2 + self.c,
            "resp": self.p * 2 + z // 4,
        }, z

    def other_core(self):
        return {"prompt": self.zl * 2 + (1 - self.c)}

    def along(self, axis, d):
        return self.plane(d, 0)[0] if axis == 0 else self.plane(0, d)[0]


class Spread:
    def __init__(self, at, buf, axis, send, recv, base, forward=None):
        self.at = at
        self.buf = buf
        self.axis = axis
        self.a = at.x if axis == 0 else at.y
        self.b = at.y if axis == 0 else at.x
        self.send = send
        self.recv = recv
        self.base = base
        self.sent = []
        self.forward = forward or (lambda ref, step: None)

    def copy(self, src, dst, sem, device):
        return pltpu.make_async_remote_copy(
            src_ref=src,
            dst_ref=dst,
            send_sem=self.send.at[self.base + sem],
            recv_sem=self.recv.at[self.base + sem],
            device_id=device,
            device_id_type=MESH,
        )

    def push(self, ref, sem, device):
        c = self.copy(ref, ref, sem, device)
        c.start()
        self.sent.append(c)

    def take(self, ref, sem, device):
        self.copy(ref, ref, sem, device).wait_recv()

    def first(self):
        mine = self.buf.at[self.a, self.b]
        for d in (1, 3, 2):
            self.push(mine, d - 1, self.at.along(1 - self.axis, d))

    def second(self):
        for d in (1, 3, 2):
            self.take(
                self.buf.at[self.a, lax.rem(self.b + 4 - d, 4)],
                d - 1,
                self.at.along(1 - self.axis, d),
            )
        row = self.buf.at[self.a]
        self.push(row, 3, self.at.along(self.axis, 1))
        self.push(row, 4, self.at.along(self.axis, 3))
        self.forward(row, 0)

    def relay(self):
        low = lax.rem(self.a + 3, 4)
        high = lax.rem(self.a + 1, 4)
        self.take(self.buf.at[low], 3, self.at.along(self.axis, 1))
        self.push(self.buf.at[low, pl.ds(0, 2)], 5, self.at.along(self.axis, 1))
        self.forward(self.buf.at[low], 1)
        self.take(self.buf.at[high], 4, self.at.along(self.axis, 3))
        self.push(self.buf.at[high, pl.ds(2, 2)], 6, self.at.along(self.axis, 3))
        self.forward(self.buf.at[high], 2)

    def finish(self):
        far = lax.rem(self.a + 2, 4)
        self.take(self.buf.at[far, pl.ds(0, 2)], 5, self.at.along(self.axis, 1))
        self.take(self.buf.at[far, pl.ds(2, 2)], 6, self.at.along(self.axis, 3))
        self.forward(self.buf.at[far], 3)

    def drain(self):
        for c in self.sent:
            c.wait_send()


SPREAD_SEMS = 7
HOLD_SEMS = 9


class Hold:
    def __init__(self, at, raw, sel, out, send, recv, base):
        self.at = at
        self.raw = raw
        self.sel = sel
        self.out = out
        self.send = send
        self.recv = recv
        self.base = base
        self.par = lax.rem(at.x + at.y, 2)
        self.sent = []

    def copy(self, src, dst, sem, device):
        return pltpu.make_async_remote_copy(
            src_ref=src,
            dst_ref=dst,
            send_sem=self.send.at[self.base + sem],
            recv_sem=self.recv.at[self.base + sem],
            device_id=device,
            device_id_type=MESH,
        )

    def spot(self, par, x, y):
        return par, par * (x // 2) + (1 - par) * (y // 2)

    def mine(self):
        return self.raw.at[self.spot(self.par, self.at.x, self.at.y)]

    def columns(self, x):
        return self.out.at[lax.rem(x, 2), x // 2, lax.rem(x, 2)]

    def rows(self, y):
        return self.out.at[1 - lax.rem(y, 2), :, lax.rem(y, 2), y // 2]

    def first(self):
        mine = self.mine()
        for d in (1, 3, 2):
            c = self.copy(mine, mine, d - 1, self.at.plane(d * self.par, d * (1 - self.par))[0])
            c.start()
            self.sent.append(c)

    def second(self, picks, own):
        at = self.at
        for d in (1, 3, 2):
            par = lax.rem(self.par + d, 2)
            x = lax.rem(at.x + (4 - d) * par, 4)
            y = lax.rem(at.y + (4 - d) * (1 - par), 4)
            spot = self.raw.at[self.spot(par, x, y)]
            self.copy(spot, spot, d - 1, at.along(0, d)).wait_recv()
        for d in (1, 3, 2):
            for axis in range(2):
                p = picks(axis, d)
                self.sel[axis, d - 1] = self.raw[axis, :, 0] * p[0] + self.raw[axis, :, 1] * p[1]
                target = self.columns(at.x) if axis == 0 else self.rows(at.y)
                c = self.copy(self.sel.at[axis, d - 1], target, 3 + axis * 3 + d - 1, at.along(axis, d))
                c.start()
                self.sent.append(c)
        chosen = [self.raw[axis, :, 0] * own[0] + self.raw[axis, :, 1] * own[1] for axis in range(2)]
        self.out[lax.rem(at.x, 2), at.x // 2, lax.rem(at.x, 2)] = chosen[0]
        for i in range(2):
            self.out[1 - lax.rem(at.y, 2), i, lax.rem(at.y, 2), at.y // 2] = chosen[1][i]

    def finish(self):
        at = self.at
        for d in (1, 3, 2):
            spot = self.columns(lax.rem(at.x + 4 - d, 4))
            self.copy(spot, spot, 3 + d - 1, at.along(0, d)).wait_recv()
            spot = self.rows(lax.rem(at.y + 4 - d, 4))
            self.copy(spot, spot, 6 + d - 1, at.along(1, d)).wait_recv()

    def drain(self):
        for c in self.sent:
            c.wait_send()


def step_kernel(
    dims,
    ph_hbm, pk_hbm, pv_hbm, rh_hbm, rq_hbm, rk_hbm, rv_hbm, cot_hbm,
    rew_ref, rp_ref, rl_ref, pt_ref, qd_hbm, qu_hbm, vd_hbm, vu_hbm,
    attn_ref, gath,
    ph, rh, qd, vd, rq_ref, rk_ref, rv_ref, cot_ref, qu_ref, vu_ref,
    k_raw, v_raw, k_sel, v_sel, k_all, v_all,
    s_scr, e_scr, v_scr, m_scr, l_scr, o_scr, dq_scr,
    stat, stat_in,
    rsb, rsr, bs32, bs16, bz_in,
    g_send, g_in, zbuf, tags, acc32, acc16, core_in, vterm,
    load_sem, h_send, h_recv, sp_send, sp_recv, z_send, z_recv, st_send, st_recv,
    rs_send, rs_recv, bz_sem, g_ssem, g_rsem, zl_ssem, zl_rsem, tag_ssem, tag_rsem, c_sem, f_sem,
):
    (D, HD, HQ, R, T, PB, RL) = dims
    at = Place()
    rows = RL * HQ
    qtiles = (D + HQ * HD) // HD
    dtiles = D // HD
    per = qtiles // SIDE
    half_t = T // 2

    barrier = pltpu.get_barrier_semaphore()

    def greet_plane(k, _):
        pl.semaphore_signal(
            barrier, inc=1, device_id=at.plane(k // 4, lax.rem(k, 4))[0], device_id_type=MESH
        )
        return 0

    def greet_line(k, _):
        pl.semaphore_signal(barrier, inc=1, device_id=at.line(k)[0], device_id_type=MESH)
        return 0

    lax.fori_loop(1, SIDE, greet_plane, 0)
    lax.fori_loop(1, NZ, greet_line, 0)
    pl.semaphore_signal(barrier, inc=1, device_id=at.other_core(), device_id_type=MESH)

    par = lax.rem(at.x + at.y, 2)
    place = par * (at.x // 2) + (1 - par) * (at.y // 2)
    loads = [
        pltpu.make_async_copy(s, d, load_sem.at[i])
        for i, (s, d) in enumerate(
            (
                (pk_hbm, k_raw.at[0, par, place]),
                (pv_hbm, v_raw.at[0, par, place, :, pl.ds(0, PB)]),
                (ph_hbm, ph),
                (vd_hbm, vd),
                (rh_hbm, rh),
                (qd_hbm, qd),
                (rq_hbm, rq_ref),
                (qu_hbm, qu_ref),
                (vu_hbm, vu_ref),
                (rk_hbm, rk_ref),
                (rv_hbm, rv_ref),
                (cot_hbm, cot_ref),
            )
        )
    ]
    for c in loads:
        c.start()

    for s in range(2):
        v_raw[0, par, place, s, PB : PB + R, :] = jnp.zeros((R, HD), BF16)
    rsb[...] = jnp.zeros(rsb.shape, BF16)
    for t in range(dtiles + 1, qtiles):
        for s in range(2):
            g_send[1, t // per, s, t % per] = jnp.zeros((R, HD), BF16)

    chosen = rp_ref[0, 0]
    length = rl_ref[0, 0]
    reward = rew_ref[0, 0]
    pick = [(chosen == s).astype(F32) for s in range(2)]
    ten = [pt_ref[0], pt_ref[1]]
    own_ten = jnp.where(chosen == 0, ten[0], ten[1])

    row8 = lax.broadcasted_iota(jnp.int32, (8, HD), 0)
    stat[0] = jnp.where(
        row8 == 0,
        reward * pick[0],
        jnp.where(
            row8 == 1,
            reward * pick[1],
            jnp.where(row8 == 2, pick[0], jnp.where(row8 == 3, pick[1], 0.0)),
        ),
    )

    loads[0].wait()
    pl.semaphore_wait(barrier, SIDE - 1 + NZ - 1 + 1)

    def hold(raw, sel, out, z, i):
        return Hold(at, raw.at[z], sel.at[z], out.at[z], h_send, h_recv, i * HOLD_SEMS)

    ko, kp = [hold(k_raw, k_sel, k_all, z, z) for z in range(2)]
    vo, vp = [hold(v_raw, v_sel, v_all, z, 2 + z) for z in range(2)]
    partner = at.line(4)[0]

    def across(raw, i):
        return pltpu.make_async_remote_copy(
            src_ref=raw.at[0, par, place], dst_ref=raw.at[1, par, place],
            send_sem=z_send.at[i], recv_sem=z_recv.at[i],
            device_id=partner, device_id_type=MESH,
        )

    zk = across(k_raw, 0)
    zv = across(v_raw, 1)
    zk.start()
    ko.first()

    def stat_copy(step, d):
        i = step * 3 + d - 1
        device = partner if step == 2 else at.along(step, d)
        return pltpu.make_async_remote_copy(
            src_ref=stat.at[step], dst_ref=stat_in.at[i],
            send_sem=st_send.at[i], recv_sem=st_recv.at[i],
            device_id=device, device_id_type=MESH,
        )

    def pick_copy(d):
        return pltpu.make_async_remote_copy(
            src_ref=stat.at[0], dst_ref=stat_in.at[6 + d],
            send_sem=st_send.at[6 + d], recv_sem=st_recv.at[6 + d],
            device_id=at.along(1, d), device_id_type=MESH,
        )

    stat_copies = [[stat_copy(0, d) for d in (1, 2, 3)], [stat_copy(1, d) for d in (1, 2, 3)], [stat_copy(2, 1)]]
    pick_copies = [pick_copy(d) for d in (1, 2, 3)]

    def stat_start(step):
        for c in stat_copies[step]:
            c.start()

    def stat_sum(step):
        total = stat[step]
        for i, c in enumerate(stat_copies[step]):
            c.wait_recv()
            total = total + stat_in[step * 3 + i]
        stat[step + 1] = total

    def picks(axis, d):
        tile = stat_in[(0 if axis == 0 else 7) + 3 - d].astype(BF16)
        return [tile[2 + s : 3 + s] for s in range(2)]

    own_pick = [stat[0].astype(BF16)[2 + s : 3 + s] for s in range(2)]

    stat_start(0)
    for c in pick_copies:
        c.start()
    for i in (1, 2, 3):
        loads[i].wait()
    for s in range(2):
        low = dot_nt(vd[ten[s]], ph[s]).astype(BF16)
        v_raw[0, par, place, s, PB : PB + R, 0:PB] = low

    vo.first()
    zv.start()

    r16 = lax.broadcasted_iota(jnp.int32, (R, HD), 0)
    owner = jnp.where(r16 < T, ten[0], ten[1])
    mask = (owner == lax.rem(r16, T)).astype(F32).astype(BF16)

    tags[at.z] = mask

    def tag_copy(k, sender):
        spot = tags.at[sender]
        return pltpu.make_async_remote_copy(
            src_ref=spot, dst_ref=spot, send_sem=tag_ssem.at[k], recv_sem=tag_rsem.at[k],
            device_id=at.line(k)[0], device_id_type=MESH,
        )

    def tag_start(k, _):
        tag_copy(k, at.z).start()
        return 0

    def tag_wait(k, _):
        tag_copy(k, at.z).wait_send()
        tag_copy(k, lax.rem(at.z + NZ - k, NZ)).wait_recv()
        return 0

    for c in loads[4:]:
        c.wait()
    low_qv = dot_nt(jnp.concatenate([qd[own_ten], vd[own_ten]], axis=0), rh[...]).astype(BF16)
    low_q = low_qv[0:R]
    low_v = low_qv[R : 2 * R]
    q_up = qu_ref[own_ten]
    v_up = vu_ref[own_ten]
    queries = (rq_ref[...].astype(F32) + 2.0 * dot_tn(low_q, q_up)).astype(BF16)
    own_val = (rv_ref[...].astype(F32) + 2.0 * dot_tn(low_v, v_up)).astype(BF16)
    qh = jnp.concatenate([queries[:, h * HD : (h + 1) * HD] for h in range(HQ)], axis=0)
    rk = rk_ref[...]
    stat_sum(0)
    for c in pick_copies:
        c.wait_recv()
    ko.second(picks, own_pick)
    stat_start(1)
    vo.second(picks, own_pick)

    factor = HD ** (-0.5) * LOG2E
    s_own = dot_nt(qh, rk)
    q_pos = lax.rem(lax.broadcasted_iota(jnp.int32, (rows, RL), 0), RL)
    k_pos = lax.broadcasted_iota(jnp.int32, (rows, RL), 1)
    allowed = (k_pos <= q_pos) & (k_pos < length)
    m_own = jnp.max(jnp.where(allowed, s_own, -1e30), axis=1, keepdims=True)

    zk.wait_recv()
    kp.first()
    lax.fori_loop(1, NZ, tag_start, 0)
    stat_sum(1)
    stat_start(2)
    ko.finish()

    cols = 4 * PB
    row_r = lax.broadcasted_iota(jnp.int32, (R, HD), 0)
    col_r = lax.broadcasted_iota(jnp.int32, (R, HD), 1)
    lift = jnp.concatenate(
        [2.0 * v_up.astype(F32), (row_r == col_r).astype(F32)], axis=1
    ).astype(BF16)

    def keys(c):
        return k_all[c // 4, (c % 4) // 2, c % 2].reshape(cols, HD)

    def low_rows(c):
        return jnp.concatenate(
            [v_all[c // 4, (c % 4) // 2, c % 2, j // 2, j % 2, PB : PB + R, :] for j in range(4)], axis=1
        )

    def scores(half, start):
        m_scr[...] = jnp.broadcast_to(start, (rows, HD))
        for c in range(4 * half, 4 * half + 4):
            sc = dot_nt(qh, keys(c))
            s_scr[c] = sc
            top = sc[:, 0:HD]
            for j in range(1, cols // HD):
                top = jnp.maximum(top, sc[:, j * HD : (j + 1) * HD])
            m_scr[...] = jnp.maximum(m_scr[...], top)
        top = jnp.max(m_scr[...], axis=1, keepdims=True) * factor
        m_scr[...] = jnp.broadcast_to(top, (rows, HD))
        return top

    def exps(half):
        l_scr[...] = jnp.zeros((rows, HD), F32)
        for c in range(4 * half, 4 * half + 4):
            sc = s_scr[c]
            mb = m_scr[...]
            part = l_scr[...]
            for j in range(cols // HD):
                ex = jnp.exp2(sc[:, j * HD : (j + 1) * HD] * factor - mb)
                part = part + ex
                e_scr[c, :, j * HD : (j + 1) * HD] = ex.astype(BF16)
            l_scr[...] = part
        return jnp.sum(l_scr[...], axis=1, keepdims=True)

    def values(half):
        for c in range(4 * half, 4 * half + 4):
            ext = dot_tn(low_rows(c), lift)
            blk = v_all[c // 4, (c % 4) // 2, c % 2, :, :, 0:PB, :].reshape(4, PB, HD)
            for j in range(4):
                v_scr[c, j * PB : (j + 1) * PB, 0:HD] = (
                    blk[j].astype(F32) + ext[j * HD : j * HD + PB, 0:HD]
                ).astype(BF16)
                v_scr[c, j * PB : (j + 1) * PB, HD : 2 * HD] = ext[
                    j * HD : j * HD + PB, HD : 2 * HD
                ].astype(BF16)
            o_scr[half] += dot_nn(e_scr[c], v_scr[c])

    top0 = scores(0, m_own)
    kp.second(picks, own_pick)
    l0 = exps(0)
    e_own = jnp.where(allowed, jnp.exp2(s_own * factor - top0), 0.0)
    e_own16 = e_own.astype(BF16)
    l0 = l0 + jnp.sum(e_own, axis=1, keepdims=True)
    zv.wait_recv()
    vp.first()
    o_scr[0, :, 0:HD] = dot_nn(e_own16, own_val)
    o_scr[0, :, HD : 2 * HD] = jnp.zeros((rows, HD), F32)
    o_scr[1] = jnp.zeros((rows, 2 * HD), F32)
    vo.finish()
    values(0)

    stat_sum(2)
    st = stat[3]
    mean = pick[0] * st[0:1] / jnp.maximum(st[2:3], 1.0) + pick[1] * st[1:2] / jnp.maximum(st[3:4], 1.0)
    weight = -(reward - mean) / RL
    live = (lax.broadcasted_iota(jnp.int32, (RL, HD), 0) < length).astype(F32) * weight
    ct = cot_ref[...].astype(F32)
    up = jnp.concatenate(
        [(ct[:, h * HD : (h + 1) * HD] * live).astype(BF16) for h in range(HQ)], axis=0
    )
    up32 = up.astype(F32)

    kp.finish()
    top1 = scores(1, jnp.full((rows, 1), -1e30, F32))
    vp.second(picks, own_pick)
    l1 = exps(1)
    top = jnp.maximum(top0, top1)
    share0 = jnp.exp2(top0 - top)
    share1 = jnp.exp2(top1 - top)
    inv = 1.0 / (share0 * l0 + share1 * l1)
    scale = [share0 * inv, share1 * inv]
    un = [(up32 * scale[h]).astype(BF16) for h in range(2)]

    for c in range(8):
        half = c // 4
        if c % 4 == 0:
            uv = dot_nt(v_up, un[half]).astype(BF16)
        x = (c % 2) * 2 + (c % 4) // 2
        back = dot_nn(uv, e_scr[c])
        z = at.zh if half == 0 else 1 - at.zh
        for j in range(4):
            y = (j % 2) * 2 + j // 2
            piece = back[:, j * PB : (j + 1) * PB]
            for s in range(2):
                rsb[x * 4 + y, z, s, :, 0:PB] = (piece * pick[s]).astype(BF16)

    def plane_copy(src, dst, send, recv, k):
        device, p = at.plane(k // 4, lax.rem(k, 4))
        return pltpu.make_async_remote_copy(
            src_ref=src.at[p], dst_ref=dst.at[k], send_sem=send.at[k], recv_sem=recv.at[k],
            device_id=device, device_id_type=MESH,
        )

    def plane_start(src, dst, send, recv):
        def body(k, _):
            plane_copy(src, dst, send, recv, k).start()
            return 0

        lax.fori_loop(1, SIDE, body, 0)

    def plane_sum(src, dst, send, recv):
        def body(k, total):
            plane_copy(src, dst, send, recv, k).wait_recv()
            return total + dst[k].astype(F32)

        return lax.fori_loop(1, SIDE, body, src[at.p].astype(F32))

    def plane_drain(src, dst, send, recv):
        def body(k, _):
            plane_copy(src, dst, send, recv, k).wait_send()
            return 0

        lax.fori_loop(1, SIDE, body, 0)

    back_set = (rsb, rsr, rs_send, rs_recv)
    grad_set = [(g_send.at[i], g_in.at[i], g_ssem.at[i], g_rsem.at[i]) for i in range(2)]
    plane_start(*back_set)

    dov = dot_tn(e_own16, un[0]).astype(BF16)
    vb = dot_nt(v_up, dov).astype(BF16)
    vterm[...] = 2.0 * dot_nn(vb, rh[...])
    for c in range(4):
        s_scr[c] = dot_nt(un[0], v_scr[c, :, 0:HD])
    vp.finish()
    values(1)

    attended = o_scr[0, :, 0:HD] * scale[0] + o_scr[1, :, 0:HD] * scale[1]
    for h in range(HQ):
        attn_ref[:, h * HD : (h + 1) * HD] = attended[h * RL : (h + 1) * RL].astype(BF16)
    delta = jnp.sum(up32 * attended, axis=1, keepdims=True)

    total_back = plane_sum(*back_set)
    bs32[...] = total_back
    bs16[...] = total_back.astype(BF16)
    bz = pltpu.make_async_remote_copy(
        src_ref=bs16.at[1 - at.zh], dst_ref=bz_in, send_sem=bz_sem.at[0], recv_sem=bz_sem.at[1],
        device_id=partner, device_id_type=MESH,
    )
    bz.start()

    ds_own = (e_own * (dot_nt(un[0], own_val) - delta * scale[0])).astype(BF16)
    dq_scr[...] = dot_nn(ds_own, rk)
    for c in range(8):
        half = c // 4
        if c % 4 == 0:
            m_scr[...] = jnp.broadcast_to(delta * scale[half], (rows, HD))
        e16 = e_scr[c]
        dp = s_scr[c] if half == 0 else dot_nt(un[1], v_scr[c, :, 0:HD])
        db = m_scr[...]
        ds = jnp.concatenate(
            [
                (
                    e16[:, j * HD : (j + 1) * HD].astype(F32)
                    * (dp[:, j * HD : (j + 1) * HD] - db)
                ).astype(BF16)
                for j in range(cols // HD)
            ],
            axis=1,
        )
        dq_scr[...] += dot_nn(ds, keys(c))

    dq = (dq_scr[...] * (HD ** (-0.5))).astype(BF16)
    dq_wide = jnp.concatenate([dq[h * RL : (h + 1) * RL] for h in range(HQ)], axis=1)
    qb = dot_nt(q_up, dq_wide).astype(BF16)
    down = 2.0 * dot_nn(qb, rh[...])
    q_term_up = 2.0 * dot_nn(low_q, dq_wide)
    for t in range(qtiles):
        if t < dtiles:
            tile = down[:, t * HD : (t + 1) * HD]
        else:
            tile = q_term_up[:, (t - dtiles) * HD : (t - dtiles + 1) * HD]
        for s in range(2):
            g_send[0, t // per, s, t % per] = (tile * pick[s]).astype(BF16)
    plane_start(*grad_set[0])

    vup_term = 2.0 * (
        dot_tn(o_scr[0, :, HD : HD + R].astype(BF16), un[0])
        + dot_tn(o_scr[1, :, HD : HD + R].astype(BF16), un[1])
        + dot_nn(low_v, dov)
    )
    for s in range(2):
        g_send[1, dtiles // per, s, dtiles % per] = (vup_term * pick[s]).astype(BF16)
    bz.wait_recv()
    back = (bs32[at.zh] + bz_in[...].astype(F32)).astype(BF16)
    for s in range(2):
        term = 2.0 * dot_nn(back[s][:, 0:PB], ph[s]) + vterm[...] * pick[s]
        for t in range(dtiles):
            g_send[1, t // per, s, t % per] = term[:, t * HD : (t + 1) * HD].astype(BF16)
    plane_start(*grad_set[1])

    def line_copy(i, k, sender):
        device, _ = at.line(k)
        spot = zbuf.at[i, sender]
        return pltpu.make_async_remote_copy(
            src_ref=spot, dst_ref=spot, send_sem=zl_ssem.at[i, k], recv_sem=zl_rsem.at[i, k],
            device_id=device, device_id_type=MESH,
        )

    def line_start(i):
        total = plane_sum(*grad_set[i]).astype(BF16)
        zbuf[i, at.z] = total.reshape(2 * per, R, HD)

        def body(k, _):
            line_copy(i, k, at.z).start()
            return 0

        lax.fori_loop(1, NZ, body, 0)

    def core_copy(i):
        return pltpu.make_async_remote_copy(
            src_ref=acc16.at[i, 1 - at.c], dst_ref=core_in.at[i], send_sem=c_sem.at[i, 0],
            recv_sem=c_sem.at[i, 1], device_id=at.other_core(), device_id_type=MESH,
        )

    def line_sum(i):
        def waits(k, _):
            line_copy(i, k, lax.rem(at.z + NZ - k, NZ)).wait_recv()
            return 0

        lax.fori_loop(1, NZ, waits, 0)
        tag = [tags[z].astype(F32) for z in range(NZ)]
        for j in range(per):
            data = [[zbuf[i, z, n * per + j].astype(F32) for n in range(2)] for z in range(NZ)]
            for t in range(T):
                part = sum(
                    data[z][n] * tag[z][n * T + t : n * T + t + 1] for z in range(NZ) for n in range(2)
                )
                acc32[i, t // half_t, t % half_t, j] = part
                acc16[i, t // half_t, t % half_t, j] = part.astype(BF16)
        core_copy(i).start()

    forwards = []

    def make_forward(i, h):
        def forward(ref, step):
            c = pltpu.make_async_remote_copy(
                src_ref=ref, dst_ref=ref, send_sem=f_sem.at[i, h, step, 0],
                recv_sem=f_sem.at[i, h, step, 1], device_id=at.other_core(), device_id_type=MESH,
            )
            c.start()
            forwards.append(c)

        return forward

    streams = [
        [
            Spread(
                at, gath.at[i, at.c, h], h, sp_send, sp_recv, (i * 2 + h) * SPREAD_SEMS,
                make_forward(i, h),
            )
            for h in range(2)
        ]
        for i in range(2)
    ]

    def gather_start(i):
        core_copy(i).wait_recv()
        final = (acc32[i, at.c] + core_in[i].astype(F32)).astype(BF16)
        for h in range(2):
            a, b = (at.x, at.y) if h == 0 else (at.y, at.x)
            gath[i, at.c, h, a, b] = final[2 * h : 2 * h + 2]
            streams[i][h].first()

    def gather_second(i):
        for h in range(2):
            streams[i][h].second()

    def gather_relay(i):
        for h in range(2):
            streams[i][h].relay()

    def gather_finish(i):
        for h in range(2):
            streams[i][h].finish()

    def gather_out(i):
        for h in range(2):
            g = streams[i][h]
            for step, d in enumerate((0, 3, 1, 2)):
                row = gath.at[i, 1 - at.c, h, lax.rem(g.a + d, 4)]
                pltpu.make_async_remote_copy(
                    src_ref=row, dst_ref=row, send_sem=f_sem.at[i, h, step, 0],
                    recv_sem=f_sem.at[i, h, step, 1], device_id=at.other_core(),
                    device_id_type=MESH,
                ).wait_recv()

    lax.fori_loop(1, NZ, tag_wait, 0)
    line_start(0)
    line_start(1)
    line_sum(0)
    line_sum(1)
    gather_start(0)
    gather_start(1)
    gather_second(0)
    gather_second(1)
    gather_relay(0)
    gather_relay(1)
    gather_finish(0)
    gather_finish(1)
    gather_out(0)
    gather_out(1)

    for c in [zk, zv, bz] + pick_copies + [c for step in stat_copies for c in step] + forwards:
        c.wait_send()
    for g in [ko, kp, vo, vp] + streams[0] + streams[1]:
        g.drain()
    plane_drain(*back_set)
    for i in range(2):
        plane_drain(*grad_set[i])

        def body(k, _):
            line_copy(i, k, at.z).wait_send()
            return 0

        lax.fori_loop(1, NZ, body, 0)
        core_copy(i).wait_send()


def widen_kernel(
    dims, gath, attn_in, attn_out, qd_out, qu_out, vd_out, vu_out,
    qd, qu, vd, vu, out_sem, attn_sem,
):
    (D, HD, HQ, R, T, PB, RL) = dims
    qtiles = (D + HQ * HD) // HD
    dtiles = D // HD
    per = qtiles // SIDE
    attn = pltpu.make_async_copy(attn_in, attn_out, attn_sem)
    parts = [(i, c, h) for c in range(2) for h in range(2) for i in range(2)]
    attn.start()
    stores = []
    for k, (i, c, h) in enumerate(parts):
        down, up = (qd, qu) if i == 0 else (vd, vu)
        down_out, up_out = (qd_out, qu_out) if i == 0 else (vd_out, vu_out)
        first = c * 4 + h * 2
        for t in range(qtiles):
            if i == 1 and t > dtiles:
                continue
            p, j = t // per, t % per
            a, b = (p // 4, p % 4) if h == 0 else (p % 4, p // 4)
            tile = gath[i, c, h, a, b, :, j].astype(F32)
            if t < dtiles:
                down[first : first + 2, :, t * HD : (t + 1) * HD] = tile
            else:
                up[first : first + 2, :, (t - dtiles) * HD : (t - dtiles + 1) * HD] = tile
        pair = pl.ds(first, 2)
        for n, (src, dst) in enumerate(((down, down_out), (up, up_out))):
            store = pltpu.make_async_copy(src.at[pair], dst.at[pair], out_sem.at[2 * k + n])
            store.start()
            stores.append(store)
    for store in stores:
        store.wait()
    attn.wait()


def per_device(
    prompt_hidden, prompt_keys, prompt_values, resp_hidden, resp_queries, resp_keys, resp_values,
    cotangent, rewards, resp_prompt, resp_len, prompt_tenant, q_down, q_up, v_down, v_up,
):
    D = prompt_hidden.shape[2]
    PB = prompt_hidden.shape[1]
    HD = prompt_keys.shape[2]
    HQ = resp_queries.shape[2] // HD
    T, _, R = q_down.shape
    RL = resp_hidden.shape[1]
    dims = (D, HD, HQ, R, T, PB, RL)
    rows = RL * HQ
    per = (D + HQ * HD) // HD // SIDE
    cols = 4 * PB
    vmem = pl.BlockSpec(memory_space=pltpu.VMEM)
    smem = pl.BlockSpec(memory_space=pltpu.SMEM)
    hbm = pl.BlockSpec(memory_space=pl.ANY)
    dma = pltpu.SemaphoreType.DMA
    gath_shape = (2, 2, 2, 4, 4, 2, per, R, HD)
    attn, gath = pl.pallas_call(
        functools.partial(step_kernel, dims),
        name="step",
        out_shape=(
            pltpu.VMEM((RL, HQ * HD), BF16),
            pltpu.VMEM(gath_shape, BF16),
        ),
        in_specs=[hbm] * 8 + [smem] * 4 + [hbm] * 4,
        out_specs=(vmem, vmem),
        scratch_shapes=[
            pltpu.VMEM((2, PB, D), BF16),
            pltpu.VMEM((RL, D), BF16),
            pltpu.VMEM((T, R, D), BF16),
            pltpu.VMEM((T, R, D), BF16),
            pltpu.VMEM((RL, HQ * HD), BF16),
            pltpu.VMEM((RL, HD), BF16),
            pltpu.VMEM((RL, HD), BF16),
            pltpu.VMEM((RL, HQ * HD), BF16),
            pltpu.VMEM((T, R, HQ * HD), BF16),
            pltpu.VMEM((T, R, HD), BF16),
            pltpu.VMEM((2, 2, 2, 2, PB, HD), BF16),
            pltpu.VMEM((2, 2, 2, 2, PB + R, HD), BF16),
            pltpu.VMEM((2, 2, 3, 2, PB, HD), BF16),
            pltpu.VMEM((2, 2, 3, 2, PB + R, HD), BF16),
            pltpu.VMEM((2, 2, 2, 2, 2, PB, HD), BF16),
            pltpu.VMEM((2, 2, 2, 2, 2, PB + R, HD), BF16),
            pltpu.VMEM((8, rows, cols), F32),
            pltpu.VMEM((8, rows, cols), BF16),
            pltpu.VMEM((8, cols, 2 * HD), BF16),
            pltpu.VMEM((rows, HD), F32),
            pltpu.VMEM((rows, HD), F32),
            pltpu.VMEM((2, rows, 2 * HD), F32),
            pltpu.VMEM((rows, HD), F32),
            pltpu.VMEM((4, 8, HD), F32),
            pltpu.VMEM((10, 8, HD), F32),
            pltpu.VMEM((SIDE, 2, 2, R, HD), BF16),
            pltpu.VMEM((SIDE, 2, 2, R, HD), BF16),
            pltpu.VMEM((2, 2, R, HD), F32),
            pltpu.VMEM((2, 2, R, HD), BF16),
            pltpu.VMEM((2, R, HD), BF16),
            pltpu.VMEM((2, SIDE, 2, per, R, HD), BF16),
            pltpu.VMEM((2, SIDE, 2, per, R, HD), BF16),
            pltpu.VMEM((2, NZ, 2 * per, R, HD), BF16),
            pltpu.VMEM((NZ, R, HD), BF16),
            pltpu.VMEM((2, 2, T // 2, per, R, HD), F32),
            pltpu.VMEM((2, 2, T // 2, per, R, HD), BF16),
            pltpu.VMEM((2, T // 2, per, R, HD), BF16),
            pltpu.VMEM((R, D), F32),
            dma((12,)),
            dma((4 * HOLD_SEMS,)),
            dma((4 * HOLD_SEMS,)),
            dma((4 * SPREAD_SEMS,)),
            dma((4 * SPREAD_SEMS,)),
            dma((2,)),
            dma((2,)),
            dma((10,)),
            dma((10,)),
            dma((SIDE,)),
            dma((SIDE,)),
            dma((2,)),
            dma((2, SIDE)),
            dma((2, SIDE)),
            dma((2, NZ)),
            dma((2, NZ)),
            dma((NZ,)),
            dma((NZ,)),
            dma((2, 2)),
            dma((2, 2, 4, 2)),
        ],
        compiler_params=pltpu.CompilerParams(
            collective_id=0, has_side_effects=True, vmem_limit_bytes=58 * 2**20
        ),
    )(
        prompt_hidden, prompt_keys, prompt_values, resp_hidden[0], resp_queries[0], resp_keys[0],
        resp_values[0], cotangent[0], rewards, resp_prompt, resp_len, prompt_tenant,
        jnp.swapaxes(q_down, 1, 2), q_up, jnp.swapaxes(v_down, 1, 2), v_up,
    )

    shapes = ((T, R, D), (T, R, HQ * HD), (T, R, D), (T, R, HD))
    attn, qd_t, g_qu, vd_t, g_vu = pl.pallas_call(
        functools.partial(widen_kernel, dims),
        name="widen",
        out_shape=(jax.ShapeDtypeStruct((RL, HQ * HD), BF16),)
        + tuple(jax.ShapeDtypeStruct(x, F32) for x in shapes),
        in_specs=[vmem, vmem],
        out_specs=(hbm,) * 5,
        scratch_shapes=[pltpu.VMEM(x, F32) for x in shapes]
        + [dma((16,)), dma],
        compiler_params=pltpu.CompilerParams(vmem_limit_bytes=40 * 2**20),
    )(gath, attn)
    return (
        attn[None],
        jnp.swapaxes(qd_t, 1, 2),
        g_qu,
        jnp.swapaxes(vd_t, 1, 2),
        g_vu,
    )


def solution(mesh):
    rows = P("prompt", "resp", None)
    pair = P("prompt", "resp")
    return jax.shard_map(
        per_device,
        mesh=mesh,
        in_specs=(rows,) * 8 + (pair,) * 3 + (P("prompt"),) + (P(),) * 4,
        out_specs=(rows, P(), P(), P(), P()),
        check_vma=False,
    )
```
